256 devices in a mesh: tm: 16 (over z_lo, y, core), rows: 16 (over x, z_hi).
Axes of the slice: x: 4, y: 4, z: 8 (z_hi: 4, z_lo: 2; z = z_hi * 2 + z_lo), core: 2. Of those that a mesh axis runs over, the one named last changes fastest.
Arguments:
- queries: bfloat16 [32, 64, 32, 1536], P('tm', 'rows'), may hold values from -8 to 8
- keys: bfloat16 [32, 64, 32, 1536], P('tm', 'rows'), may hold values from -8 to 8
- values: bfloat16 [32, 64, 32, 1536], P('tm', 'rows'), may hold values from -6 to 6
- win_off: int32 [8, 8, 4, 3], replicated, may hold values from -1 to 1
- row_valid: int32 [8], replicated, may hold values from 1 to 8
Outputs:
- attended: bfloat16 [32, 64, 32, 1536], P('tm', 'rows')
The draws below stay inside these ranges and needn't reach their ends.
All inputs are finite; a program needn't handle non-finite values.
Results may differ from the reference program's by a relative error of at most 0.0047.
Values may be sent and summed in bfloat16 or wider, within the bound.
A program may use at most 128 MiB of HBM per device.

```python
import jax
import jax.numpy as jnp
from jax import lax

HEADS = 12
HEAD_DIM = 128
D = 1536
W = 32
FRAMES = 32
ROWS = 64
TIME_TILES = 8
ROW_TILES = 8
COL_TILES = 4


def draw_queries(key, part):
    key = jax.random.fold_in(key, 11)
    return jax.random.truncated_normal(key, -6.0, 6.0, (FRAMES, ROWS, W, D), jnp.float32).astype(jnp.bfloat16)


def draw_keys(key, part):
    key = jax.random.fold_in(key, 23)
    return jax.random.truncated_normal(key, -6.0, 6.0, (FRAMES, ROWS, W, D), jnp.float32).astype(jnp.bfloat16)


def with_ends(entries, own_key, low, largest):
    spot = [jax.random.randint(jax.random.fold_in(own_key, axis), (), 0, length) for axis, length in enumerate(entries.shape)]
    longest = entries.shape.index(max(entries.shape))
    beside = spot[:longest] + [(spot[longest] + 1) % entries.shape[longest]] + spot[longest + 1:]
    return entries.at[tuple(spot)].set(low).at[tuple(beside)].set(largest)


def shard_levels(stream_key, shape, split, least, largest):
    factor_of = 1.0
    for dim, blocks in split:
        heights = jax.random.uniform(jax.random.fold_in(jax.random.fold_in(stream_key, 6), dim), (blocks,), jnp.float32, least / len(split), largest / len(split))
        factor_of = factor_of * jnp.repeat(jnp.exp(heights), shape[dim] // blocks).reshape((-1,) + (1,) * (len(shape) - 1 - dim))
    return factor_of


def normal_values(own_key, shape, width, limit, cuts=(), kind=jnp.bfloat16):
    entries = width * jax.random.normal(own_key, shape, jnp.float32)
    if cuts:
        entries = entries * shard_levels(own_key, shape, cuts, -0.22, 0.18)
    return jnp.clip(entries, -limit, limit).astype(kind)


def setup_inputs(seed: int = 0) -> dict:
    seeds = jax.random.split(jax.random.key(seed), 6)
    queries = draw_queries(jax.random.fold_in(seeds[5], 71), 0)
    keys = draw_keys(jax.random.fold_in(seeds[5], 71), 0)
    values = normal_values(seeds[2], (FRAMES, ROWS, W, D), 1.0, 6.0, ((0, 16), (1, 16)))
    win_off = with_ends(jax.random.randint(seeds[3], (TIME_TILES, ROW_TILES, COL_TILES, 3), -1, 2), jax.random.fold_in(seeds[3], 1), -1, 1).astype(jnp.int32)
    row_valid = with_ends(jax.random.randint(seeds[4], (ROW_TILES,), 1, 9), jax.random.fold_in(seeds[4], 1), 1, 8).astype(jnp.int32)
    return {"queries": queries, "keys": keys, "values": values, "win_off": win_off, "row_valid": row_valid}


def anchor(*places):
    return tuple(jnp.asarray(place).astype(jnp.int32) for place in places)


def window_allowed(offsets, tile_t, tile_r, row_valid, time_tiles):
    col_tiles = offsets.shape[0]
    step_t = jnp.arange(12, dtype=jnp.int32) // 4 - 1
    key_row = jnp.arange(24, dtype=jnp.int32)
    step_r = key_row // 8 - 1
    row_within = key_row % 8
    step_w = jnp.arange(24, dtype=jnp.int32) // 8 - 1
    time_near = tile_t + step_t
    time_ok = ((time_near >= 0) & (time_near < time_tiles))[None, :] & (step_t[None, :] * offsets[:, 0:1] >= 0)
    padded = jnp.concatenate([jnp.zeros((1,), jnp.int32), row_valid.astype(jnp.int32), jnp.zeros((1,), jnp.int32)])
    nearby_valid = lax.dynamic_slice(padded, anchor(tile_r), (3,))
    picker = (step_r[:, None] + 1) == jnp.arange(3, dtype=jnp.int32)[None, :]
    row_limit = jnp.sum(jnp.where(picker, nearby_valid[None, :], 0), axis=1)
    row_ok = (row_within < row_limit)[None, :] & (step_r[None, :] * offsets[:, 1:2] >= 0)
    col_near = jnp.arange(col_tiles, dtype=jnp.int32)[:, None] + step_w[None, :]
    col_ok = (col_near >= 0) & (col_near < col_tiles) & (step_w[None, :] * offsets[:, 2:3] >= 0)
    allowed = time_ok[:, :, None, None] & row_ok[:, None, :, None] & col_ok[:, None, None, :]
    query_ok = (jnp.arange(256, dtype=jnp.int32) // 8) % 8 < nearby_valid[1]
    return allowed.reshape(col_tiles, 6912), query_ok


def attend_tiles(query_tiles, key_windows, value_windows, allowed, query_ok):
    score_scale = 1.0 / (query_tiles.shape[-1] ** 0.5)
    query_cast = query_tiles.astype(jnp.float32)
    key_cast = key_windows.astype(jnp.float32)
    scores = jnp.einsum("nqhd,nkhd->nhqk", query_cast, key_cast) * score_scale
    scores = jnp.where(allowed[:, None, None, :], scores, -jnp.inf)
    row_max = jnp.max(scores, axis=-1, keepdims=True)
    expo = jnp.exp(scores - row_max)
    row_total = jnp.sum(expo, axis=-1)
    weights = lax.optimization_barrier(expo.astype(jnp.bfloat16))
    summed = jnp.einsum("nhqk,nkhd->nqhd", weights.astype(jnp.float32), value_windows.astype(jnp.float32))
    output_tile = summed / jnp.transpose(row_total, (0, 2, 1))[..., None]
    output_tile = jnp.where(query_ok[None, :, None, None], output_tile, 0.0)
    return output_tile.astype(jnp.bfloat16)


def reference(queries, keys, values, win_off, row_valid):
    frames, row_count, columns, channels = queries.shape
    col_tiles = columns // 8
    key_padded = jnp.pad(keys, ((4, 4), (8, 8), (8, 8), (0, 0)))
    value_padded = jnp.pad(values, ((4, 4), (8, 8), (8, 8), (0, 0)))

    def block_attend(flat_index):
        tile_t = flat_index // ROW_TILES
        tile_r = flat_index % ROW_TILES
        start = anchor(4 * tile_t, 8 * tile_r, 0, 0)
        query_block = lax.dynamic_slice(queries, start, (4, 8, columns, channels))
        query_tiles = query_block.reshape(4, 8, col_tiles, 8, HEADS, HEAD_DIM)
        query_tiles = jnp.transpose(query_tiles, (2, 0, 1, 3, 4, 5)).reshape(col_tiles, 256, HEADS, HEAD_DIM)
        key_block = lax.dynamic_slice(key_padded, start, (12, 24, columns + 16, channels))
        value_block = lax.dynamic_slice(value_padded, start, (12, 24, columns + 16, channels))
        key_windows = jnp.stack([key_block[:, :, 8 * col:8 * col + 24] for col in range(col_tiles)])
        value_windows = jnp.stack([value_block[:, :, 8 * col:8 * col + 24] for col in range(col_tiles)])
        key_windows = key_windows.reshape(col_tiles, 6912, HEADS, HEAD_DIM)
        value_windows = value_windows.reshape(col_tiles, 6912, HEADS, HEAD_DIM)
        offsets = lax.dynamic_slice(win_off, anchor(tile_t, tile_r, 0, 0), (1, 1, col_tiles, 3)).reshape(col_tiles, 3)
        allowed, query_ok = window_allowed(offsets, tile_t, tile_r, row_valid, TIME_TILES)
        output_tile = attend_tiles(query_tiles, key_windows, value_windows, allowed, query_ok)
        output_tile = output_tile.reshape(col_tiles, 4, 8, 8, channels)
        return jnp.transpose(output_tile, (1, 2, 0, 3, 4)).reshape(4, 8, columns, channels)

    blocks = lax.map(block_attend, jnp.arange(TIME_TILES * ROW_TILES, dtype=jnp.int32))
    blocks = blocks.reshape(TIME_TILES, ROW_TILES, 4, 8, columns, channels)
    return jnp.transpose(blocks, (0, 2, 1, 3, 4, 5)).reshape(frames, row_count, columns, channels)
```

```python
import jax
import jax.numpy as jnp
from jax import lax
from jax.experimental import pallas as pl
from jax.experimental.pallas import tpu as pltpu
from jax.sharding import PartitionSpec as P

HEADS = 12
HEAD_DIM = 128
LOG2E = 1.4426950408889634
SCALE = LOG2E / HEAD_DIM**0.5
BF16 = jnp.bfloat16
F32 = jnp.float32
MESH = pl.DeviceIdType.MESH
VMEM_LIMIT = 60 * 1024 * 1024


def rem(a, b):
    return lax.rem(a, jnp.int32(b))


def div(a, b):
    return lax.div(a, jnp.int32(b))


class Place:
    def __init__(self):
        tm = lax.axis_index("tm")
        rows = lax.axis_index("rows")
        self.zl = div(tm, 8)
        self.y = rem(div(tm, 2), 4)
        self.core = rem(tm, 2)
        self.x = div(rows, 4)
        self.zh = rem(rows, 4)
        self.zz = div(self.zh, 2)
        self.zp = rem(self.zh, 2)
        self.z = self.zh * 2 + self.zl
        self.t = self.core * 4 + self.y
        self.rows = rows

    def worker(self, k):
        z = rem(self.z + k, 8)
        zh, zl = div(z, 2), rem(z, 2)
        return zh, zl, (zl * 8 + self.y * 2 + self.zl, self.x * 4 + zh)

    def origin(self, k):
        i = rem(self.z + k, 8)
        zh = rem(self.zh + k // 2, 4)
        core = rem(self.core + k % 2, 2)
        return zh, core, (self.core * 8 + self.y * 2 + core, self.x * 4 + zh)

    def time_neighbour(self, step):
        t = self.t + step
        ok = (t >= 0) & (t < 8)
        t = jnp.clip(t, 0, 7)
        return ok, (self.zl * 8 + rem(t, 4) * 2 + div(t, 4), self.rows)

    def row_neighbour(self, step):
        x = self.x + step
        ok = (x >= 0) & (x < 4)
        x = jnp.clip(x, 0, 3)
        return ok, (self.zl * 8 + self.y * 2 + self.core, x * 4 + self.zh)


CHUNKS = ((0, 0, 4), (1, 0, 4), (0, 4, 3), (1, 4, 3))


def gather_kernel(q_in, k_in, v_in, kv, qs, packed, send_kv, send_y, send_x, recv_kv, recv_q, recv_y, recv_x):
    me = Place()
    times = [me.time_neighbour(s) for s in (1, -1)]
    sides = [me.row_neighbour(s) for s in (1, -1)]
    myself = me.core == me.zl

    barrier = pltpu.get_barrier_semaphore()
    expect = jnp.int32(0)
    for k in range(8):
        _, _, device = me.origin(k)
        if k == 0:
            @pl.when(jnp.logical_not(myself))
            def _():
                pl.semaphore_signal(barrier, inc=1, device_id=device, device_id_type=MESH)
        else:
            pl.semaphore_signal(barrier, inc=1, device_id=device, device_id_type=MESH)
    for ok, device in times + sides:
        @pl.when(ok)
        def _():
            pl.semaphore_signal(barrier, inc=1, device_id=device, device_id_type=MESH)
        expect = expect + ok.astype(jnp.int32)

    def pack(which, source):
        for h in range(HEADS):
            block = source[:, :, :, h * HEAD_DIM:(h + 1) * HEAD_DIM].astype(F32)
            block = block.reshape(2, 4, 4, 8, HEAD_DIM)
            block = jnp.transpose(block, (2, 1, 0, 3, 4)).reshape(4, 4, 16, HEAD_DIM)
            packed[which, h] = block.astype(BF16)

    def spread(which, first, count, recv):
        index = which * 2 + (first > 0)
        for k in range(8):
            zh, zl, device = me.worker(k)
            if first == 0:
                head, column = 3 * zh + 2 * zl, 0
            else:
                head, column = 3 * zh + 1, (2 * zl if which == 2 else zl)
            source = packed.at[which, head, pl.ds(column, count)]
            slots, rows, spot = pl.ds(first, count), pl.ds(me.zp * 4, 4), pl.ds(pl.multiple_of(me.core * 16, 16), 16)
            if which == 2:
                target = qs.at[me.zz, slots, rows, spot]
            else:
                target = kv.at[which, 1, 1 + me.zz, slots, rows, spot]
            remote = pltpu.make_async_remote_copy(
                source, target, send_kv.at[index, k], recv, device_id=device, device_id_type=MESH)
            if k == 0:
                @pl.when(myself)
                def _():
                    pltpu.make_async_copy(source, target, recv).start()

                @pl.when(jnp.logical_not(myself))
                def _():
                    remote.start()
            else:
                remote.start()

    def spread_done(which, first, count):
        index = which * 2 + (first > 0)
        source = packed.at[which, 0, pl.ds(0, count)]
        for k in range(8):
            def done():
                pltpu.make_async_copy(source, source, send_kv.at[index, k]).wait()
            if k == 0:
                pl.when(jnp.logical_not(myself))(done)
            else:
                done()

    def y_copy(c, d):
        which, first, count = CHUNKS[c]
        source = kv.at[which, 1, pl.ds(1, 2), pl.ds(first, count)]
        target = kv.at[which, 2 * d, pl.ds(1, 2), pl.ds(first, count)]
        return pltpu.make_async_remote_copy(
            source, target, send_y.at[c, d], recv_y.at[c, d], device_id=times[d][1], device_id_type=MESH)

    def x_copy(c, d, dt):
        which, first, count = CHUNKS[c]
        source = kv.at[which, dt, 2 - d, pl.ds(first, count)]
        target = kv.at[which, dt, 3 * d, pl.ds(first, count)]
        return pltpu.make_async_remote_copy(
            source, target, send_x.at[c, d, dt], recv_x.at[c, d, dt], device_id=sides[d][1], device_id_type=MESH)

    has_time = [times[1][0], times[0][0], None]

    def dt_ok(dt):
        return {0: times[1][0], 1: True, 2: times[0][0]}[dt]

    def send_x_part(c, dt):
        for d in range(2):
            @pl.when(sides[d][0] & dt_ok(dt))
            def _():
                x_copy(c, d, dt).start()

    def after_y(c):
        for d in range(2):
            @pl.when(times[1 - d][0])
            def _():
                y_copy(c, d).wait_recv()
            send_x_part(c, 2 * d)

    pack(0, k_in)
    pl.semaphore_wait(barrier, expect + 8 - myself.astype(jnp.int32))
    spread(0, 0, 4, recv_kv.at[0])
    pack(1, v_in)
    spread(1, 0, 4, recv_kv.at[1])
    spread(0, 4, 3, recv_kv.at[2])
    spread(1, 4, 3, recv_kv.at[3])
    pack(2, q_in)
    spread(2, 0, 4, recv_q.at[0])
    spread(2, 4, 2, recv_q.at[1])
    for c in range(4):
        which, first, count = CHUNKS[c]
        whole = kv.at[which, 1, pl.ds(1, 2), pl.ds(first, count)]
        pltpu.make_async_copy(whole, whole, recv_kv.at[c]).wait()
        for d in range(2):
            @pl.when(times[d][0])
            def _():
                y_copy(c, d).start()
        send_x_part(c, 1)
        if c:
            after_y(c - 1)
    after_y(3)
    for i, (first, count) in enumerate(((0, 4), (4, 2))):
        whole = qs.at[:, pl.ds(first, count)]
        pltpu.make_async_copy(whole, whole, recv_q.at[i]).wait()
    for c in range(4):
        for d in range(2):
            for dt in range(3):
                @pl.when(sides[1 - d][0] & dt_ok(dt))
                def _():
                    x_copy(c, d, dt).wait_recv()
    for c in range(4):
        for d in range(2):
            @pl.when(times[d][0])
            def _():
                y_copy(c, d).wait_send()
            for dt in range(3):
                @pl.when(sides[d][0] & dt_ok(dt))
                def _():
                    x_copy(c, d, dt).wait_send()
    for which in range(3):
        spread_done(which, 0, 4)
        spread_done(which, 4, 2 if which == 2 else 3)


def attend_kernel(offsets, row_valid, kv, qs, out, turned, scores, top, total, gathered):
    me = Place()

    def turn(i, _):
        dt, row = div(i, 4), rem(i, 4)
        for c in range(7):
            turned[dt, row, c] = kv[1, dt, row, c].reshape(256, HEAD_DIM).astype(F32).T.astype(BF16)
        return 0

    lax.fori_loop(0, 12, turn, 0)

    def limit(row):
        tile = 2 * me.x - 1 + row
        inside = (tile >= 0) & (tile < 8)
        return jnp.where(inside, row_valid[jnp.clip(tile, 0, 7)], 0)

    row_number = lax.broadcasted_iota(jnp.int32, (8, 1, 256), 0)

    def tile(r, slot, base, count, column, first):
        flat = ((me.t * 8 + 2 * me.x + r) * 4 + column) * 3
        off_t, off_r, off_c = offsets[flat], offsets[flat + 1], offsets[flat + 2]
        query = qs[r, slot].reshape(256, HEAD_DIM)
        top[...] = jnp.full((8, 256), -jnp.inf, F32)
        total[...] = jnp.zeros((8, 256), F32)
        gathered[...] = jnp.zeros((HEAD_DIM, 256), F32)

        def near(b):
            dt, dr = div(b, 3), rem(b, 3)
            when = me.t + dt - 1
            ok = (when >= 0) & (when < 8) & ((dt - 1) * off_t >= 0) & ((dr - 1) * off_r >= 0)
            valid = jnp.where(ok, limit(r + dr), 0)
            valids = [jnp.where((first + j) * off_c >= 0, valid, 0) for j in range(count)]
            return dt, r + dr, valid, valids

        def score(b, _):
            dt, row, valid, valids = near(b)

            @pl.when(valid > 0)
            def _():
                keys = kv[0, dt, row, pl.ds(base, count)].reshape(count * 256, HEAD_DIM)
                s = lax.dot_general(keys, query, (((1,), (1,)), ((), ())), preferred_element_type=F32)
                scores[b, pl.ds(0, count * 256)] = s
                best = jnp.max(s.reshape(count, 8, 4, 8, 256), axis=2)
                for j in range(count):
                    mine = jnp.where(row_number < valids[j], best[j], -jnp.inf)
                    top[...] = jnp.maximum(top[...], jnp.max(mine, axis=0))
            return 0

        lax.fori_loop(0, 9, score, 0)
        shift = jnp.max(top[...], axis=0, keepdims=True) * SCALE

        def weigh(b, _):
            dt, row, valid, valids = near(b)

            @pl.when(valid > 0)
            def _():
                for j in range(count):
                    s = scores[b, pl.ds(j * 256, 256)].reshape(8, 32, 256)
                    less = jnp.where(row_number < valids[j], shift[None], jnp.inf)
                    p = jnp.exp2(s * SCALE - less)
                    total[...] += jnp.sum(p.reshape(32, 8, 256), axis=0)
                    weights = p.reshape(256, 256).astype(BF16)
                    gathered[...] += jnp.dot(turned[dt, row, base + j], weights, preferred_element_type=F32)
            return 0

        lax.fori_loop(0, 9, weigh, 0)
        result = gathered[...] / jnp.sum(total[...], axis=0, keepdims=True)
        result = result.T.reshape(8, 32, HEAD_DIM)
        keep = lax.broadcasted_iota(jnp.int32, (8, 1, HEAD_DIM), 0) < limit(r + 1)
        out[r, slot] = jnp.where(keep, result, 0.0).astype(BF16)

    def wide(i, _):
        r, kind = div(i, 3), rem(i, 3)
        shared = kind == 2
        slot = jnp.where(shared, 5 - me.zl, 1 + kind)
        base = jnp.where(shared, 4, kind)
        column = jnp.where(shared, 1 + me.zl, 1 + kind)
        tile(r, slot, base, 3, column, -1)
        return 0

    def edge(i, _):
        r, kind = div(i, 3), rem(i, 3)
        shared = kind == 2
        right = jnp.where(shared, me.zl, kind)
        slot = jnp.where(shared, 4 + me.zl, 3 * kind)
        base = jnp.where(shared, 4 + me.zl, 2 * kind)
        tile(r, slot, base, 2, 3 * right, -right)
        return 0

    lax.fori_loop(0, 6, wide, 0)
    lax.fori_loop(0, 6, edge, 0)


def return_kernel(tiles, out, landed, send, recv):
    me = Place()
    myself = me.core == me.zl
    barrier = pltpu.get_barrier_semaphore()
    for k in range(8):
        _, _, device = me.worker(k)
        if k == 0:
            @pl.when(jnp.logical_not(myself))
            def _():
                pl.semaphore_signal(barrier, inc=1, device_id=device, device_id_type=MESH)
        else:
            pl.semaphore_signal(barrier, inc=1, device_id=device, device_id_type=MESH)
    pl.semaphore_wait(barrier, 8 - myself.astype(jnp.int32))

    def copies(k, part):
        zh, core, device = me.origin(k)
        rows, spot = pl.ds(rem(zh, 2) * 4, 4), pl.ds(pl.multiple_of(core * 16, 16), 16)
        if part == 0:
            source = tiles.at[div(zh, 2), pl.ds(0, 4), rows, spot]
            target = landed.at[3 * me.zh + 2 * me.zl]
        else:
            source = tiles.at[div(zh, 2), pl.ds(4, 2), rows, spot]
            target = landed.at[3 * me.zh + 1, pl.ds(2 * me.zl, 2)]
        return source, target, pltpu.make_async_remote_copy(
            source, target, send.at[part, k], recv.at[0], device_id=device, device_id_type=MESH)

    for part in range(2):
        for k in range(8):
            source, target, remote = copies(k, part)
            if k == 0:
                @pl.when(myself)
                def _():
                    pltpu.make_async_copy(source, target, recv.at[0]).start()

                @pl.when(jnp.logical_not(myself))
                def _():
                    remote.start()
            else:
                remote.start()
    pltpu.make_async_copy(landed, landed, recv.at[0]).wait()
    for h in range(HEADS):
        block = landed[h].astype(F32).reshape(4, 4, 2, 8, HEAD_DIM)
        block = jnp.transpose(block, (2, 1, 0, 3, 4)).reshape(2, 4, 32, HEAD_DIM)
        out[:, :, :, h * HEAD_DIM:(h + 1) * HEAD_DIM] = block.astype(BF16)
    for part in range(2):
        for k in range(8):
            def done():
                copies(k, part)[2].wait_send()
            if k == 0:
                pl.when(jnp.logical_not(myself))(done)
            else:
                done()


def vmem():
    return pl.BlockSpec(memory_space=pltpu.VMEM)


def anywhere():
    return pl.BlockSpec(memory_space=pl.ANY)


def smem():
    return pl.BlockSpec(memory_space=pltpu.SMEM)


def shards(queries, keys, values, win_off, row_valid):
    dma = pltpu.SemaphoreType.DMA
    kv, qs = pl.pallas_call(
        gather_kernel,
        out_shape=(
            jax.ShapeDtypeStruct((2, 3, 4, 7, 8, 32, HEAD_DIM), BF16),
            jax.ShapeDtypeStruct((2, 6, 8, 32, HEAD_DIM), BF16),
        ),
        in_specs=[vmem()] * 3,
        out_specs=(anywhere(), anywhere()),
        scratch_shapes=[
            pltpu.VMEM((3, HEADS, 4, 4, 16, HEAD_DIM), BF16),
            dma((6, 8)), dma((4, 2)), dma((4, 2, 3)),
            dma((4,)), dma((2,)), dma((4, 2)), dma((4, 2, 3)),
        ],
        compiler_params=pltpu.CompilerParams(
            collective_id=0, has_side_effects=True, vmem_limit_bytes=VMEM_LIMIT),
    )(queries, keys, values)
    tiles = pl.pallas_call(
        attend_kernel,
        out_shape=jax.ShapeDtypeStruct((2, 6, 8, 32, HEAD_DIM), BF16),
        in_specs=[smem(), smem(), vmem(), vmem()],
        out_specs=vmem(),
        scratch_shapes=[
            pltpu.VMEM((3, 4, 7, HEAD_DIM, 256), BF16),
            pltpu.VMEM((9, 768, 256), F32),
            pltpu.VMEM((8, 256), F32),
            pltpu.VMEM((8, 256), F32),
            pltpu.VMEM((HEAD_DIM, 256), F32),
        ],
        compiler_params=pltpu.CompilerParams(vmem_limit_bytes=VMEM_LIMIT),
    )(win_off.reshape(-1), row_valid, kv, qs)
    return pl.pallas_call(
        return_kernel,
        out_shape=jax.ShapeDtypeStruct(queries.shape, BF16),
        in_specs=[anywhere()],
        out_specs=vmem(),
        scratch_shapes=[
            pltpu.VMEM((HEADS, 4, 4, 16, HEAD_DIM), BF16),
            dma((2, 8)), dma((1,)),
        ],
        compiler_params=pltpu.CompilerParams(
            collective_id=1, has_side_effects=True, vmem_limit_bytes=VMEM_LIMIT),
    )(tiles)


def solution(mesh):
    return jax.shard_map(
        shards,
        mesh=mesh,
        in_specs=(
            P("tm", "rows", None, None),
            P("tm", "rows", None, None),
            P("tm", "rows", None, None),
            P(),
            P(),
        ),
        out_specs=P("tm", "rows", None, None),
        check_vma=False,
    )
```

```python
import jax
import jax.numpy as jnp
from jax import lax
from jax.experimental import pallas as pl
from jax.experimental.pallas import tpu as pltpu
from jax.sharding import PartitionSpec as P

HEADS = 12
HEAD_DIM = 128
LOG2E = 1.4426950408889634
SCALE = LOG2E / HEAD_DIM**0.5
BF16 = jnp.bfloat16
F32 = jnp.float32
MESH = pl.DeviceIdType.MESH
VMEM_LIMIT = 60 * 1024 * 1024


def rem(a, b):
    return lax.rem(a, jnp.int32(b))


def div(a, b):
    return lax.div(a, jnp.int32(b))


class Place:
    def __init__(self):
        tm = lax.axis_index("tm")
        rows = lax.axis_index("rows")
        self.zl = div(tm, 8)
        self.y = rem(div(tm, 2), 4)
        self.core = rem(tm, 2)
        self.x = div(rows, 4)
        self.zh = rem(rows, 4)
        self.zz = div(self.zh, 2)
        self.zp = rem(self.zh, 2)
        self.z = self.zh * 2 + self.zl
        self.t = self.core * 4 + self.y
        self.rows = rows

    def worker(self, k):
        z = rem(self.z + k, 8)
        zh, zl = div(z, 2), rem(z, 2)
        return zh, zl, (zl * 8 + self.y * 2 + self.zl, self.x * 4 + zh)

    def origin(self, k):
        i = rem(self.z + k, 8)
        zh = rem(self.zh + k // 2, 4)
        core = rem(self.core + k % 2, 2)
        return zh, core, (self.core * 8 + self.y * 2 + core, self.x * 4 + zh)

    def time_neighbour(self, step):
        t = self.t + step
        ok = (t >= 0) & (t < 8)
        t = jnp.clip(t, 0, 7)
        return ok, (self.zl * 8 + rem(t, 4) * 2 + div(t, 4), self.rows)

    def row_neighbour(self, step):
        x = self.x + step
        ok = (x >= 0) & (x < 4)
        x = jnp.clip(x, 0, 3)
        return ok, (self.zl * 8 + self.y * 2 + self.core, x * 4 + self.zh)


GROUPS = ((0, 2), (2, 2), (4, 3))
CHUNKS = tuple((which, first, count) for first, count in GROUPS for which in (0, 1))
QUERY_GROUPS = ((0, 4), (4, 2))


def kernel(offsets, row_valid, q_in, k_in, v_in, out, kv, qs, packed, tiles, landed, scores, top, total, gathered,
           send_kv, send_q, send_y, send_x, send_o, recv_kv, recv_q, recv_y, recv_x, recv_o):
    me = Place()
    times = [me.time_neighbour(s) for s in (1, -1)]
    sides = [me.row_neighbour(s) for s in (1, -1)]
    myself = me.core == me.zl
    other = jnp.logical_not(myself)

    for i, dt in ((1, 0), (0, 2)):
        @pl.when(jnp.logical_not(times[i][0]))
        def _():
            kv[:, dt] = jnp.zeros((2, 4, 7, 8, 32, HEAD_DIM), BF16)
    for i, row in ((1, 0), (0, 3)):
        @pl.when(jnp.logical_not(sides[i][0]))
        def _():
            kv[:, :, row] = jnp.zeros((2, 3, 7, 8, 32, HEAD_DIM), BF16)

    barrier = pltpu.get_barrier_semaphore()

    def greet(device):
        pl.semaphore_signal(barrier, inc=1, device_id=device, device_id_type=MESH)

    @pl.when(other)
    def _():
        greet(me.origin(0)[2])
        greet(me.worker(0)[2])

    for k in range(1, 8):
        greet(me.origin(k)[2])
        greet(me.worker(k)[2])
    expect = 16 - 2 * myself.astype(jnp.int32)
    for ok, device in times + sides:
        @pl.when(ok)
        def _():
            greet(device)
        expect = expect + ok.astype(jnp.int32)

    def pack(which, source):
        for h in range(HEADS):
            block = source[:, :, :, h * HEAD_DIM:(h + 1) * HEAD_DIM].astype(F32)
            block = block.reshape(2, 4, 4, 8, HEAD_DIM)
            block = jnp.transpose(block, (2, 1, 0, 3, 4)).reshape(4, 4, 16, HEAD_DIM)
            packed[which, h] = block.astype(BF16)

    my_rows, my_spot = pl.ds(me.zp * 4, 4), pl.ds(pl.multiple_of(me.core * 16, 16), 16)

    def share(which, first, count, send, recv, k):
        zh, zl, device = me.worker(k)
        if first < 4:
            head, column = 3 * zh + 2 * zl, first
        else:
            head, column = 3 * zh + 1, (2 * zl if which == 2 else zl)
        source = packed.at[which, head, pl.ds(column, count)]
        if which == 2:
            target = qs.at[me.zz, pl.ds(first, count), my_rows, my_spot]
        else:
            target = kv.at[which, 1, 1 + me.zz, pl.ds(first, count), my_rows, my_spot]
        return source, target, pltpu.make_async_remote_copy(
            source, target, send.at[k], recv, device_id=device, device_id_type=MESH)

    def spread(which, first, count, send, recv):
        source, target, remote = share(which, first, count, send, recv, 0)

        @pl.when(myself)
        def _():
            pltpu.make_async_copy(source, target, recv).start()

        @pl.when(other)
        def _():
            remote.start()

        def step(k, _):
            share(which, first, count, send, recv, k)[2].start()
            return 0

        lax.fori_loop(1, 8, step, 0)

    def spread_sent(which, first, count, send, recv):
        pl.when(other)(lambda: share(which, first, count, send, recv, 0)[2].wait_send())

        def step(k, _):
            share(which, first, count, send, recv, k)[2].wait_send()
            return 0

        lax.fori_loop(1, 8, step, 0)

    def chunk_share(c):
        which, first, count = CHUNKS[c]
        return which, first, count, send_kv.at[c], recv_kv.at[c]

    def query_share(i):
        first, count = QUERY_GROUPS[i]
        return 2, first, count, send_q.at[i], recv_q.at[i]

    def y_copy(c, d):
        which, first, count = CHUNKS[c]
        source = kv.at[which, 1, pl.ds(1, 2), pl.ds(first, count)]
        target = kv.at[which, 2 * d, pl.ds(1, 2), pl.ds(first, count)]
        return pltpu.make_async_remote_copy(
            source, target, send_y.at[c, d], recv_y.at[c, d], device_id=times[d][1], device_id_type=MESH)

    def x_copy(c, d, dt):
        which, first, count = CHUNKS[c]
        source = kv.at[which, dt, 2 - d, pl.ds(first, count)]
        target = kv.at[which, dt, 3 * d, pl.ds(first, count)]
        return pltpu.make_async_remote_copy(
            source, target, send_x.at[c, d, dt], recv_x.at[c, d, dt], device_id=sides[d][1], device_id_type=MESH)

    filled = (times[1][0], True, times[0][0])

    def send_x_part(c, dt):
        for d in range(2):
            pl.when(sides[d][0] & filled[dt])(lambda: x_copy(c, d, dt).start())

    def after_own(c):
        which, first, count = CHUNKS[c]
        whole = kv.at[which, 1, pl.ds(1, 2), pl.ds(first, count)]
        pltpu.make_async_copy(whole, whole, recv_kv.at[c]).wait()
        for d in range(2):
            pl.when(times[d][0])(lambda: y_copy(c, d).start())
        send_x_part(c, 1)

    def after_y(c):
        for d in range(2):
            pl.when(filled[2 * d])(lambda: y_copy(c, d).wait_recv())
            send_x_part(c, 2 * d)

    def after_x(c):
        for d in range(2):
            for dt in range(3):
                pl.when(sides[1 - d][0] & filled[dt])(lambda: x_copy(c, d, dt).wait_recv())

    def queries_here(i):
        first, count = QUERY_GROUPS[i]
        whole = qs.at[:, pl.ds(first, count)]
        pltpu.make_async_copy(whole, whole, recv_q.at[i]).wait()

    limits = []
    for row in range(4):
        tile = 2 * me.x - 1 + row
        inside = (tile >= 0) & (tile < 8)
        limits.append(jnp.where(inside, row_valid[jnp.clip(tile, 0, 7)], 0))

    def attend(wave, r, slot, base, count, column, first):
        flat = ((me.t * 8 + 2 * me.x + r) * 4 + column) * 3
        off_t, off_r, off_c = offsets[flat], offsets[flat + 1], offsets[flat + 2]
        query = qs[r, slot].reshape(256, HEAD_DIM)
        if wave == 0:
            near = [(1, 1, limits[1]), (1, 2, limits[2])]
        elif wave == 1:
            near = [(dt, row, limits[row]) for dt in (0, 2) for row in (1, 2)]
        else:
            near = [(dt, 3 * r, jnp.where(r == 0, limits[0], limits[3])) for dt in (0, 1, 2)]
        less = []
        for dt, row, valid in near:
            dr = row - r - 1
            ok = ((dt - 1) * off_t >= 0) & (dr * off_r >= 0)
            if dt != 1:
                ok = ok & filled[dt]
            for j in range(count):
                limit = jnp.where(ok & ((first + j) * off_c >= 0), valid, 0)
                less.append([jnp.where(limit > row_in, 0.0, -jnp.inf).astype(F32) for row_in in range(8)])
        best = jnp.full((8, 256), -jnp.inf, F32)
        for i, (dt, row, _) in enumerate(near):
            keys = kv[0, dt, row, pl.ds(base, count)].reshape(count * 256, HEAD_DIM)
            s = lax.dot_general(keys, query, (((1,), (1,)), ((), ())), preferred_element_type=F32)
            scores[i, pl.ds(0, count * 256)] = s
            highest = jnp.max(s.reshape(count * 8, 4, 8, 256), axis=1)
            for j in range(count):
                for n in range(8):
                    best = jnp.maximum(best, highest[j * 8 + n] + less[i * count + j][n])
        best = jnp.broadcast_to(jnp.max(best, axis=0, keepdims=True), (8, 256))
        if wave == 0:
            summed = jnp.zeros((8, 256), F32)
            held = jnp.zeros((HEAD_DIM, 256), F32)
        else:
            before = top[r, slot]
            best = jnp.maximum(best, before)
            fade = jnp.exp2((before - best) * SCALE)
            summed = total[r, slot] * fade
            held = gathered[r, slot] * fade[0:1]
        shift = best * SCALE
        for i, (dt, row, _) in enumerate(near):
            parts = []
            for j in range(count):
                for n in range(8):
                    s = scores[i, pl.ds(j * 256 + n * 32, 32)].reshape(4, 8, 256)
                    p = jnp.exp2(s * SCALE - (shift - less[i * count + j][n])[None])
                    summed = summed + jnp.sum(p, axis=0)
                    parts.append(p.reshape(32, 256).astype(BF16))
            weights = jnp.concatenate(parts, axis=0)
            value = kv[1, dt, row, pl.ds(base, count)].reshape(count * 256, HEAD_DIM)
            held = held + lax.dot_general(value, weights, (((0,), (0,)), ((), ())), preferred_element_type=F32)
        if wave < 2:
            top[r, slot] = best
            total[r, slot] = summed
            gathered[r, slot] = held
        else:
            result = held / jnp.sum(summed, axis=0, keepdims=True)
            result = result.T.reshape(8, 32, HEAD_DIM)
            keep = lax.broadcasted_iota(jnp.int32, (8, 1, HEAD_DIM), 0) < jnp.where(r == 0, limits[1], limits[2])
            tiles[r, slot] = jnp.where(keep, result, 0.0).astype(BF16)

    def whole_head(wave):
        def step(i, _):
            r, right = div(i, 2), rem(i, 2)
            attend(wave, r, 1 + right, right, 3, 1 + right, -1)
            attend(wave, r, 3 * right, 2 * right, 2, 3 * right, -right)
            return 0

        lax.fori_loop(0, 4, step, 0)

    def shared_head(wave):
        def step(r, _):
            attend(wave, r, 5 - me.zl, 4, 3, 1 + me.zl, -1)
            attend(wave, r, 4 + me.zl, 4 + me.zl, 2, 3 * me.zl, -me.zl)
            return 0

        lax.fori_loop(0, 2, step, 0)

    def result_share(part, k):
        zh, core, device = me.origin(k)
        rows, spot = pl.ds(rem(zh, 2) * 4, 4), pl.ds(pl.multiple_of(core * 16, 16), 16)
        if part == 0:
            source = tiles.at[div(zh, 2), pl.ds(0, 4), rows, spot]
            target = landed.at[3 * me.zh + 2 * me.zl]
        else:
            source = tiles.at[div(zh, 2), pl.ds(4, 2), rows, spot]
            target = landed.at[3 * me.zh + 1, pl.ds(2 * me.zl, 2)]
        return source, target, pltpu.make_async_remote_copy(
            source, target, send_o.at[part, k], recv_o.at[part], device_id=device, device_id_type=MESH)

    def give_back(part):
        source, target, remote = result_share(part, 0)

        @pl.when(myself)
        def _():
            pltpu.make_async_copy(source, target, recv_o.at[part]).start()

        @pl.when(other)
        def _():
            remote.start()

        def step(k, _):
            result_share(part, k)[2].start()
            return 0

        lax.fori_loop(1, 8, step, 0)

    def given_back(part):
        pl.when(other)(lambda: result_share(part, 0)[2].wait_send())

        def step(k, _):
            result_share(part, k)[2].wait_send()
            return 0

        lax.fori_loop(1, 8, step, 0)

    def unpack(part):
        heads = [h for h in range(HEADS) if (h % 3 == 1) == (part == 1)]
        whole = landed.at[pl.ds(0, 8 if part == 0 else 4)]
        pltpu.make_async_copy(whole, whole, recv_o.at[part]).wait()
        for h in heads:
            block = landed[h].astype(F32).reshape(4, 4, 2, 8, HEAD_DIM)
            block = jnp.transpose(block, (2, 1, 0, 3, 4)).reshape(2, 4, 32, HEAD_DIM)
            out[:, :, :, h * HEAD_DIM:(h + 1) * HEAD_DIM] = block.astype(BF16)

    pack(0, k_in)
    pl.semaphore_wait(barrier, expect)
    spread(*chunk_share(0))
    pack(1, v_in)
    spread(*chunk_share(1))
    spread(*chunk_share(2))
    spread(*chunk_share(3))
    pack(2, q_in)
    spread(*query_share(0))
    spread(*chunk_share(4))
    spread(*chunk_share(5))
    spread(*query_share(1))
    for c in range(4):
        after_own(c)
        if c:
            after_y(c - 1)
    after_y(3)
    queries_here(0)
    whole_head(0)
    after_own(4)
    whole_head(1)
    after_y(4)
    after_own(5)
    for c in range(4):
        after_x(c)
    after_y(5)
    whole_head(2)
    give_back(0)
    queries_here(1)
    shared_head(0)
    shared_head(1)
    after_x(4)
    after_x(5)
    shared_head(2)
    give_back(1)
    unpack(0)
    unpack(1)
    for c in range(6):
        spread_sent(*chunk_share(c))
        for d in range(2):
            pl.when(times[d][0])(lambda: y_copy(c, d).wait_send())
            for dt in range(3):
                pl.when(sides[d][0] & filled[dt])(lambda: x_copy(c, d, dt).wait_send())
    for i in range(2):
        spread_sent(*query_share(i))
        given_back(i)


def shards(queries, keys, values, win_off, row_valid):
    dma = pltpu.SemaphoreType.DMA
    smem = pl.BlockSpec(memory_space=pltpu.SMEM)
    vmem = pl.BlockSpec(memory_space=pltpu.VMEM)
    return pl.pallas_call(
        kernel,
        out_shape=jax.ShapeDtypeStruct(queries.shape, BF16),
        in_specs=[smem, smem, vmem, vmem, vmem],
        out_specs=vmem,
        scratch_shapes=[
            pltpu.VMEM((2, 3, 4, 7, 8, 32, HEAD_DIM), BF16),
            pltpu.VMEM((2, 6, 8, 32, HEAD_DIM), BF16),
            pltpu.VMEM((3, HEADS, 4, 4, 16, HEAD_DIM), BF16),
            pltpu.VMEM((2, 6, 8, 32, HEAD_DIM), BF16),
            pltpu.VMEM((HEADS, 4, 4, 16, HEAD_DIM), BF16),
            pltpu.VMEM((4, 768, 256), F32),
            pltpu.VMEM((2, 6, 8, 256), F32),
            pltpu.VMEM((2, 6, 8, 256), F32),
            pltpu.VMEM((2, 6, HEAD_DIM, 256), F32),
            dma((6, 8)), dma((2, 8)), dma((6, 2)), dma((6, 2, 3)), dma((2, 8)),
            dma((6,)), dma((2,)), dma((6, 2)), dma((6, 2, 3)), dma((2,)),
        ],
        compiler_params=pltpu.CompilerParams(
            collective_id=0, has_side_effects=True, vmem_limit_bytes=VMEM_LIMIT),
    )(win_off.reshape(-1), row_valid, queries, keys, values)


def solution(mesh):
    return jax.shard_map(
        shards,
        mesh=mesh,
        in_specs=(
            P("tm", "rows", None, None),
            P("tm", "rows", None, None),
            P("tm", "rows", None, None),
            P(),
            P(),
        ),
        out_specs=P("tm", "rows", None, None),
        check_vma=False,
    )
```

```python
import jax
import jax.numpy as jnp
from jax import lax
from jax.experimental import pallas as pl
from jax.experimental.pallas import tpu as pltpu
from jax.sharding import PartitionSpec as P

HEADS = 12
HEAD_DIM = 128
LOG2E = 1.4426950408889634
SCALE = LOG2E / HEAD_DIM**0.5
BF16 = jnp.bfloat16
F32 = jnp.float32
MESH = pl.DeviceIdType.MESH
VMEM_LIMIT = 60 * 1024 * 1024


def rem(a, b):
    return lax.rem(a, jnp.int32(b))


def div(a, b):
    return lax.div(a, jnp.int32(b))


class Place:
    def __init__(self):
        tm = lax.axis_index("tm")
        rows = lax.axis_index("rows")
        self.zl = div(tm, 8)
        self.y = rem(div(tm, 2), 4)
        self.core = rem(tm, 2)
        self.x = div(rows, 4)
        self.zh = rem(rows, 4)
        self.zz = div(self.zh, 2)
        self.zp = rem(self.zh, 2)
        self.z = self.zh * 2 + self.zl
        self.t = self.core * 4 + self.y
        self.rows = rows

    def worker(self, k):
        z = rem(self.z + k, 8)
        zh, zl = div(z, 2), rem(z, 2)
        return zh, zl, (zl * 8 + self.y * 2 + self.zl, self.x * 4 + zh)

    def origin(self, k):
        i = rem(self.z + k, 8)
        zh = rem(self.zh + k // 2, 4)
        core = rem(self.core + k % 2, 2)
        return zh, core, (self.core * 8 + self.y * 2 + core, self.x * 4 + zh)

    def time_neighbour(self, step):
        t = self.t + step
        ok = (t >= 0) & (t < 8)
        t = jnp.clip(t, 0, 7)
        return ok, (self.zl * 8 + rem(t, 4) * 2 + div(t, 4), self.rows)

    def row_neighbour(self, step):
        x = self.x + step
        ok = (x >= 0) & (x < 4)
        x = jnp.clip(x, 0, 3)
        return ok, (self.zl * 8 + self.y * 2 + self.core, x * 4 + self.zh)


GROUPS = ((0, 2), (2, 2), (4, 3))
CHUNKS = tuple((which, first, count) for first, count in GROUPS for which in (0, 1))
QUERY_GROUPS = ((0, 4), (4, 2))
ROWS_FIRST = 5


def kernel(offsets, row_valid, q_in, k_in, v_in, landed, kv, qs, packed, tiles, scores, top, total, gathered,
           send_kv, send_q, send_y, send_x, send_c, send_o, recv_kv, recv_q, recv_y, recv_x, recv_c, recv_o):
    me = Place()
    times = [me.time_neighbour(s) for s in (1, -1)]
    sides = [me.row_neighbour(s) for s in (1, -1)]
    myself = me.core == me.zl
    other = jnp.logical_not(myself)

    for i, dt in ((1, 0), (0, 2)):
        @pl.when(jnp.logical_not(times[i][0]))
        def _():
            kv[:, dt] = jnp.zeros((2, 4, 7, 8, 32, HEAD_DIM), BF16)
    for i, row in ((1, 0), (0, 3)):
        @pl.when(jnp.logical_not(sides[i][0]))
        def _():
            kv[:, :, row] = jnp.zeros((2, 3, 7, 8, 32, HEAD_DIM), BF16)

    barrier = pltpu.get_barrier_semaphore()

    def greet(device):
        pl.semaphore_signal(barrier, inc=1, device_id=device, device_id_type=MESH)

    @pl.when(other)
    def _():
        greet(me.origin(0)[2])
        greet(me.worker(0)[2])

    for k in range(1, 8):
        greet(me.origin(k)[2])
        greet(me.worker(k)[2])
    expect = 16 - 2 * myself.astype(jnp.int32)
    for ok, device in times + sides:
        @pl.when(ok)
        def _():
            greet(device)
        expect = expect + ok.astype(jnp.int32)

    def pack(which, source):
        for h in range(HEADS):
            block = source[:, :, :, h * HEAD_DIM:(h + 1) * HEAD_DIM].astype(F32)
            block = block.reshape(2, 4, 4, 8, HEAD_DIM)
            block = jnp.transpose(block, (2, 1, 0, 3, 4)).reshape(4, 4, 16, HEAD_DIM)
            packed[which, h] = block.astype(BF16)

    my_rows, my_spot = pl.ds(me.zp * 4, 4), pl.ds(pl.multiple_of(me.core * 16, 16), 16)

    def share(which, first, count, send, recv, k):
        zh, zl, device = me.worker(k)
        if first < 4:
            head, column = 3 * zh + 2 * zl, first
        else:
            head, column = 3 * zh + 1, (2 * zl if which == 2 else zl)
        source = packed.at[which, head, pl.ds(column, count)]
        if which == 2:
            target = qs.at[me.zz, pl.ds(first, count), my_rows, my_spot]
        else:
            target = kv.at[which, 1, 1 + me.zz, pl.ds(first, count), my_rows, my_spot]
        return source, target, pltpu.make_async_remote_copy(
            source, target, send.at[k], recv, device_id=device, device_id_type=MESH)

    def spread(which, first, count, send, recv):
        source, target, remote = share(which, first, count, send, recv, 0)

        @pl.when(myself)
        def _():
            pltpu.make_async_copy(source, target, recv).start()

        @pl.when(other)
        def _():
            remote.start()

        def step(k, _):
            share(which, first, count, send, recv, k)[2].start()
            return 0

        lax.fori_loop(1, 8, step, 0)

    def spread_sent(which, first, count, send, recv):
        pl.when(other)(lambda: share(which, first, count, send, recv, 0)[2].wait_send())

        def step(k, _):
            share(which, first, count, send, recv, k)[2].wait_send()
            return 0

        lax.fori_loop(1, 8, step, 0)

    def chunk_share(c):
        which, first, count = CHUNKS[c]
        return which, first, count, send_kv.at[c], recv_kv.at[c]

    def query_share(i):
        first, count = QUERY_GROUPS[i]
        return 2, first, count, send_q.at[i], recv_q.at[i]

    def y_copy(c, d):
        which, first, count = CHUNKS[c]
        source = kv.at[which, 1, pl.ds(1, 2), pl.ds(first, count)]
        target = kv.at[which, 2 * d, pl.ds(1, 2), pl.ds(first, count)]
        return pltpu.make_async_remote_copy(
            source, target, send_y.at[c, d], recv_y.at[c, d], device_id=times[d][1], device_id_type=MESH)

    def x_copy(c, d, dt):
        which, first, count = CHUNKS[c]
        source = kv.at[which, dt, 2 - d, pl.ds(first, count)]
        target = kv.at[which, dt, 3 * d, pl.ds(first, count)]
        return pltpu.make_async_remote_copy(
            source, target, send_x.at[c, d, dt], recv_x.at[c, d, dt], device_id=sides[d][1], device_id_type=MESH)

    filled = (times[1][0], True, times[0][0])

    def send_x_part(c, dt):
        for d in range(2):
            pl.when(sides[d][0] & filled[dt])(lambda: x_copy(c, d, dt).start())

    def after_own(c):
        which, first, count = CHUNKS[c]
        whole = kv.at[which, 1, pl.ds(1, 2), pl.ds(first, count)]
        pltpu.make_async_copy(whole, whole, recv_kv.at[c]).wait()
        for d in range(2):
            pl.when(times[d][0])(lambda: y_copy(c, d).start())
        send_x_part(c, 1)

    def after_y(c):
        for d in range(2):
            pl.when(filled[2 * d])(lambda: y_copy(c, d).wait_recv())
            send_x_part(c, 2 * d)

    def after_x(c):
        for d in range(2):
            for dt in range(3):
                pl.when(sides[1 - d][0] & filled[dt])(lambda: x_copy(c, d, dt).wait_recv())

    def corner_copy(d, side):
        which, first, count = CHUNKS[ROWS_FIRST]
        source = kv.at[which, 1, 3 * side, pl.ds(first, count)]
        target = kv.at[which, 2 * d, 3 * side, pl.ds(first, count)]
        return pltpu.make_async_remote_copy(
            source, target, send_c.at[d, side], recv_c.at[d, side], device_id=times[d][1], device_id_type=MESH)

    def send_corners():
        for side in range(2):
            here = sides[1 - side][0]
            pl.when(here)(lambda: x_copy(ROWS_FIRST, side, 1).wait_recv())
            for d in range(2):
                pl.when(here & times[d][0])(lambda: corner_copy(d, side).start())

    def own_y_here():
        for d in range(2):
            pl.when(filled[2 * d])(lambda: y_copy(ROWS_FIRST, d).wait_recv())

    def corners_here():
        for side in range(2):
            for d in range(2):
                pl.when(sides[1 - side][0] & filled[2 * d])(lambda: corner_copy(d, side).wait_recv())

    def queries_here(i):
        first, count = QUERY_GROUPS[i]
        whole = qs.at[:, pl.ds(first, count)]
        pltpu.make_async_copy(whole, whole, recv_q.at[i]).wait()

    limits = []
    for row in range(4):
        tile = 2 * me.x - 1 + row
        inside = (tile >= 0) & (tile < 8)
        limits.append(jnp.where(inside, row_valid[jnp.clip(tile, 0, 7)], 0))

    def attend(wave, r, slot, base, count, column, first):
        off_t, off_r, off_c = [offsets[me.t, i, column, 2 * me.x + r] for i in range(3)]
        query = qs[r, slot].reshape(256, HEAD_DIM)
        if wave == 0:
            near = [(1, 1, limits[1]), (1, 2, limits[2])]
        elif wave == 1:
            near = [(dt, row, limits[row]) for dt in (0, 2) for row in (1, 2)]
        else:
            near = [(dt, 3 * r, jnp.where(r == 0, limits[0], limits[3])) for dt in (0, 1, 2)]
        less = []
        for dt, row, valid in near:
            dr = row - r - 1
            ok = ((dt - 1) * off_t >= 0) & (dr * off_r >= 0)
            if dt != 1:
                ok = ok & filled[dt]
            for j in range(count):
                limit = jnp.where(ok & ((first + j) * off_c >= 0), valid, 0)
                less.append([jnp.where(limit > row_in, 0.0, -jnp.inf).astype(F32) for row_in in range(8)])
        best = jnp.full((8, 256), -jnp.inf, F32)
        for i, (dt, row, _) in enumerate(near):
            keys = kv[0, dt, row, pl.ds(base, count)].reshape(count * 256, HEAD_DIM)
            s = lax.dot_general(keys, query, (((1,), (1,)), ((), ())), preferred_element_type=F32)
            scores[i, pl.ds(0, count * 256)] = s
            highest = jnp.max(s.reshape(count * 8, 4, 8, 256), axis=1)
            for j in range(count):
                for n in range(8):
                    best = jnp.maximum(best, highest[j * 8 + n] + less[i * count + j][n])
        best = jnp.broadcast_to(jnp.max(best, axis=0, keepdims=True), (8, 256))
        if wave == 0:
            summed = jnp.zeros((8, 256), F32)
            held = jnp.zeros((HEAD_DIM, 256), F32)
        else:
            before = top[r, slot]
            best = jnp.maximum(best, before)
            fade = jnp.exp2((before - best) * SCALE)
            summed = total[r, slot] * fade
            held = gathered[r, slot] * fade[0:1]
        shift = best * SCALE
        for i, (dt, row, _) in enumerate(near):
            parts = []
            for j in range(count):
                for n in range(8):
                    s = scores[i, pl.ds(j * 256 + n * 32, 32)].reshape(4, 8, 256)
                    p = jnp.exp2(s * SCALE - (shift - less[i * count + j][n])[None])
                    summed = summed + jnp.sum(p, axis=0)
                    parts.append(p.reshape(32, 256).astype(BF16))
            weights = jnp.concatenate(parts, axis=0)
            value = kv[1, dt, row, pl.ds(base, count)].reshape(count * 256, HEAD_DIM)
            held = held + lax.dot_general(value, weights, (((0,), (0,)), ((), ())), preferred_element_type=F32)
        if wave < 2:
            top[r, slot] = best
            total[r, slot] = summed
            gathered[r, slot] = held
        else:
            result = held / jnp.sum(summed, axis=0, keepdims=True)
            result = result.T.reshape(8, 32, HEAD_DIM)
            keep = lax.broadcasted_iota(jnp.int32, (8, 1, HEAD_DIM), 0) < jnp.where(r == 0, limits[1], limits[2])
            tiles[r, slot] = jnp.where(keep, result, 0.0).astype(BF16)

    def whole_head(wave, then=None):
        def step(r, _):
            def half(right, _):
                attend(wave, r, 1 + right, right, 3, 1 + right, -1)
                attend(wave, r, 3 * right, 2 * right, 2, 3 * right, -right)
                return 0

            lax.fori_loop(0, 2, half, 0)
            if then is not None:
                then(r)
            return 0

        lax.fori_loop(0, 2, step, 0)

    def shared_head(wave, then=None):
        def step(r, _):
            attend(wave, r, 5 - me.zl, 4, 3, 1 + me.zl, -1)
            attend(wave, r, 4 + me.zl, 4 + me.zl, 2, 3 * me.zl, -me.zl)
            if then is not None:
                then(r)
            return 0

        lax.fori_loop(0, 2, step, 0)

    def result_share(part, r, j):
        zp, core = rem(me.zp + div(j, 2), 2), rem(me.core + rem(j, 2), 2)
        device = (me.core * 8 + me.y * 2 + core, me.x * 4 + r * 2 + zp)
        rows, spot = pl.ds(zp * 4, 4), pl.ds(pl.multiple_of(core * 16, 16), 16)
        if part == 0:
            source = tiles.at[r, pl.ds(0, 4), rows, spot]
            target = landed.at[3 * me.zh + 2 * me.zl]
        else:
            source = tiles.at[r, pl.ds(4, 2), rows, spot]
            target = landed.at[3 * me.zh + 1, pl.ds(2 * me.zl, 2)]
        return source, target, pltpu.make_async_remote_copy(
            source, target, send_o.at[part, r, j], recv_o.at[part], device_id=device, device_id_type=MESH)

    def give_back(part, r):
        mine = myself & (r == me.zz)
        source, target, remote = result_share(part, r, jnp.int32(0))

        @pl.when(mine)
        def _():
            pltpu.make_async_copy(source, target, recv_o.at[part]).start()

        @pl.when(jnp.logical_not(mine))
        def _():
            remote.start()

        def step(j, _):
            result_share(part, r, j)[2].start()
            return 0

        lax.fori_loop(1, 4, step, 0)

    def given_back(part):
        def each(r, _):
            mine = myself & (r == me.zz)
            pl.when(jnp.logical_not(mine))(lambda: result_share(part, r, jnp.int32(0))[2].wait_send())

            def step(j, _):
                result_share(part, r, j)[2].wait_send()
                return 0

            lax.fori_loop(1, 4, step, 0)
            return 0

        lax.fori_loop(0, 2, each, 0)

    def landed_here(part):
        whole = landed.at[pl.ds(0, 8 if part == 0 else 4)]
        pltpu.make_async_copy(whole, whole, recv_o.at[part]).wait()

    pack(0, k_in)
    pl.semaphore_wait(barrier, expect)
    spread(*chunk_share(0))
    pack(1, v_in)
    spread(*chunk_share(1))
    spread(*chunk_share(2))
    spread(*chunk_share(3))
    pack(2, q_in)
    spread(*query_share(0))
    spread(*chunk_share(4))
    spread(*chunk_share(5))
    spread(*query_share(1))
    for c in range(4):
        after_own(c)
        if c:
            after_y(c - 1)
    after_y(3)
    queries_here(0)
    whole_head(0)
    whole_head(1, lambda r: pl.when(r == 0)(lambda: after_own(4)))
    after_y(4)
    after_own(5)
    for c in range(4):
        after_x(c)
    whole_head(2, lambda r: give_back(0, r))
    send_corners()
    queries_here(1)
    shared_head(0)
    own_y_here()
    shared_head(1)
    after_x(4)
    corners_here()
    shared_head(2, lambda r: give_back(1, r))
    landed_here(0)
    landed_here(1)
    for c in range(6):
        spread_sent(*chunk_share(c))
        for d in range(2):
            pl.when(times[d][0])(lambda: y_copy(c, d).wait_send())
            for dt in ((1,) if c == ROWS_FIRST else range(3)):
                pl.when(sides[d][0] & filled[dt])(lambda: x_copy(c, d, dt).wait_send())
    for i in range(2):
        spread_sent(*query_share(i))
        given_back(i)
        for d in range(2):
            pl.when(sides[1 - i][0] & times[d][0])(lambda: corner_copy(d, i).wait_send())


def unpack_kernel(landed, out):
    for h in range(HEADS):
        block = landed[h].astype(F32).reshape(4, 4, 2, 8, HEAD_DIM)
        block = jnp.transpose(block, (2, 1, 0, 3, 4)).reshape(2, 4, 32, HEAD_DIM)
        out[:, :, :, h * HEAD_DIM:(h + 1) * HEAD_DIM] = block.astype(BF16)


def shards(queries, keys, values, win_off, row_valid):
    dma = pltpu.SemaphoreType.DMA
    smem = pl.BlockSpec(memory_space=pltpu.SMEM)
    vmem = pl.BlockSpec(memory_space=pltpu.VMEM)
    landed = pl.pallas_call(
        kernel,
        out_shape=jax.ShapeDtypeStruct((HEADS, 4, 4, 16, HEAD_DIM), BF16),
        in_specs=[smem, smem, vmem, vmem, vmem],
        out_specs=pl.BlockSpec(memory_space=pl.ANY),
        scratch_shapes=[
            pltpu.VMEM((2, 3, 4, 7, 8, 32, HEAD_DIM), BF16),
            pltpu.VMEM((2, 6, 8, 32, HEAD_DIM), BF16),
            pltpu.VMEM((3, HEADS, 4, 4, 16, HEAD_DIM), BF16),
            pltpu.VMEM((2, 6, 8, 32, HEAD_DIM), BF16),
            pltpu.VMEM((4, 768, 256), F32),
            pltpu.VMEM((2, 6, 8, 256), F32),
            pltpu.VMEM((2, 6, 8, 256), F32),
            pltpu.VMEM((2, 6, HEAD_DIM, 256), F32),
            dma((6, 8)), dma((2, 8)), dma((6, 2)), dma((6, 2, 3)), dma((2, 2)), dma((2, 2, 4)),
            dma((6,)), dma((2,)), dma((6, 2)), dma((6, 2, 3)), dma((2, 2)), dma((2,)),
        ],
        compiler_params=pltpu.CompilerParams(
            collective_id=0, has_side_effects=True, vmem_limit_bytes=VMEM_LIMIT),
    )(jnp.transpose(win_off, (0, 3, 2, 1)), row_valid, queries, keys, values)
    return pl.pallas_call(
        unpack_kernel,
        out_shape=jax.ShapeDtypeStruct(queries.shape, BF16),
        in_specs=[vmem],
        out_specs=vmem,
    )(landed)


def solution(mesh):
    return jax.shard_map(
        shards,
        mesh=mesh,
        in_specs=(
            P("tm", "rows", None, None),
            P("tm", "rows", None, None),
            P("tm", "rows", None, None),
            P(),
            P(),
        ),
        out_specs=P("tm", "rows", None, None),
        check_vma=False,
    )
```

```python
import jax
import jax.numpy as jnp
from jax import lax
from jax.experimental import pallas as pl
from jax.experimental.pallas import tpu as pltpu
from jax.sharding import PartitionSpec as P

HEADS = 12
HEAD_DIM = 128
LOG2E = 1.4426950408889634
SCALE = LOG2E / HEAD_DIM**0.5
BF16 = jnp.bfloat16
F32 = jnp.float32
MESH = pl.DeviceIdType.MESH
VMEM_LIMIT = 60 * 1024 * 1024


def rem(a, b):
    return lax.rem(a, jnp.int32(b))


def div(a, b):
    return lax.div(a, jnp.int32(b))


class Place:
    def __init__(self):
        tm = lax.axis_index("tm")
        rows = lax.axis_index("rows")
        self.zl = div(tm, 8)
        self.y = rem(div(tm, 2), 4)
        self.core = rem(tm, 2)
        self.x = div(rows, 4)
        self.zh = rem(rows, 4)
        self.zz = div(self.zh, 2)
        self.zp = rem(self.zh, 2)
        self.z = self.zh * 2 + self.zl
        self.t = self.core * 4 + self.y
        self.rows = rows

    def worker(self, k):
        z = rem(self.z + k, 8)
        zh, zl = div(z, 2), rem(z, 2)
        return zh, zl, (zl * 8 + self.y * 2 + self.zl, self.x * 4 + zh)

    def origin(self, k):
        i = rem(self.z + k, 8)
        zh = rem(self.zh + k // 2, 4)
        core = rem(self.core + k % 2, 2)
        return zh, core, (self.core * 8 + self.y * 2 + core, self.x * 4 + zh)

    def time_neighbour(self, step):
        t = self.t + step
        ok = (t >= 0) & (t < 8)
        t = jnp.clip(t, 0, 7)
        return ok, (self.zl * 8 + rem(t, 4) * 2 + div(t, 4), self.rows)

    def row_neighbour(self, step):
        x = self.x + step
        ok = (x >= 0) & (x < 4)
        x = jnp.clip(x, 0, 3)
        return ok, (self.zl * 8 + self.y * 2 + self.core, x * 4 + self.zh)


GROUPS = ((0, 2), (2, 2), (6, 1), (4, 2))
CHUNKS = tuple((which, first, count) for which, (first, count) in (
    (0, GROUPS[0]), (1, GROUPS[0]), (0, GROUPS[1]), (1, GROUPS[1]),
    (0, GROUPS[2]), (0, GROUPS[3]), (1, GROUPS[2]), (1, GROUPS[3])))
QUERY_GROUPS = ((0, 4), (4, 2))
ROWS_FIRST = (4, 6)


def kernel(offsets, row_valid, q_in, k_in, v_in, landed, kv, qs, packed, tiles, scores, top, total, gathered,
           send_kv, send_q, send_y, send_x, send_c, send_o, recv_kv, recv_q, recv_y, recv_x, recv_c, recv_o):
    me = Place()
    times = [me.time_neighbour(s) for s in (1, -1)]
    sides = [me.row_neighbour(s) for s in (1, -1)]
    myself = me.core == me.zl
    other = jnp.logical_not(myself)

    for i, dt in ((1, 0), (0, 2)):
        @pl.when(jnp.logical_not(times[i][0]))
        def _():
            kv[:, dt] = jnp.zeros((2, 4, 7, 8, 32, HEAD_DIM), BF16)
    for i, row in ((1, 0), (0, 3)):
        @pl.when(jnp.logical_not(sides[i][0]))
        def _():
            kv[:, :, row] = jnp.zeros((2, 3, 7, 8, 32, HEAD_DIM), BF16)

    barrier = pltpu.get_barrier_semaphore()

    def greet(device):
        pl.semaphore_signal(barrier, inc=1, device_id=device, device_id_type=MESH)

    @pl.when(other)
    def _():
        greet(me.origin(0)[2])
        greet(me.worker(0)[2])

    for k in range(1, 8):
        greet(me.origin(k)[2])
        greet(me.worker(k)[2])
    expect = 16 - 2 * myself.astype(jnp.int32)
    for ok, device in times + sides:
        @pl.when(ok)
        def _():
            greet(device)
        expect = expect + ok.astype(jnp.int32)

    def pack(which, source):
        for h in range(HEADS):
            block = source[:, :, :, h * HEAD_DIM:(h + 1) * HEAD_DIM].astype(F32)
            block = block.reshape(2, 4, 4, 8, HEAD_DIM)
            block = jnp.transpose(block, (2, 1, 0, 3, 4)).reshape(4, 4, 16, HEAD_DIM)
            packed[which, h] = block.astype(BF16)

    my_rows, my_spot = pl.ds(me.zp * 4, 4), pl.ds(pl.multiple_of(me.core * 16, 16), 16)

    def share(which, first, count, send, recv, k):
        zh, zl, device = me.worker(k)
        if first < 4:
            head, column = 3 * zh + 2 * zl, first
        else:
            head, column = 3 * zh + 1, (2 * zl if which == 2 else zl) + first - 4
        source = packed.at[which, head, pl.ds(column, count)]
        if which == 2:
            target = qs.at[me.zz, pl.ds(first, count), my_rows, my_spot]
        else:
            target = kv.at[which, 1, 1 + me.zz, pl.ds(first, count), my_rows, my_spot]
        return source, target, pltpu.make_async_remote_copy(
            source, target, send.at[k], recv, device_id=device, device_id_type=MESH)

    def spread(which, first, count, send, recv):
        source, target, remote = share(which, first, count, send, recv, 0)

        @pl.when(myself)
        def _():
            pltpu.make_async_copy(source, target, recv).start()

        @pl.when(other)
        def _():
            remote.start()

        def step(k, _):
            share(which, first, count, send, recv, k)[2].start()
            return 0

        lax.fori_loop(1, 8, step, 0)

    def spread_sent(which, first, count, send, recv):
        pl.when(other)(lambda: share(which, first, count, send, recv, 0)[2].wait_send())

        def step(k, _):
            share(which, first, count, send, recv, k)[2].wait_send()
            return 0

        lax.fori_loop(1, 8, step, 0)

    def chunk_share(c):
        which, first, count = CHUNKS[c]
        return which, first, count, send_kv.at[c], recv_kv.at[c]

    def query_share(i):
        first, count = QUERY_GROUPS[i]
        return 2, first, count, send_q.at[i], recv_q.at[i]

    def y_copy(c, d):
        which, first, count = CHUNKS[c]
        source = kv.at[which, 1, pl.ds(1, 2), pl.ds(first, count)]
        target = kv.at[which, 2 * d, pl.ds(1, 2), pl.ds(first, count)]
        return pltpu.make_async_remote_copy(
            source, target, send_y.at[c, d], recv_y.at[c, d], device_id=times[d][1], device_id_type=MESH)

    def x_copy(c, d, dt):
        which, first, count = CHUNKS[c]
        source = kv.at[which, dt, 2 - d, pl.ds(first, count)]
        target = kv.at[which, dt, 3 * d, pl.ds(first, count)]
        return pltpu.make_async_remote_copy(
            source, target, send_x.at[c, d, dt], recv_x.at[c, d, dt], device_id=sides[d][1], device_id_type=MESH)

    filled = (times[1][0], True, times[0][0])

    def send_x_part(c, dt):
        for d in range(2):
            pl.when(sides[d][0] & filled[dt])(lambda: x_copy(c, d, dt).start())

    def after_own(c):
        which, first, count = CHUNKS[c]
        whole = kv.at[which, 1, pl.ds(1, 2), pl.ds(first, count)]
        pltpu.make_async_copy(whole, whole, recv_kv.at[c]).wait()
        for d in range(2):
            pl.when(times[d][0])(lambda: y_copy(c, d).start())
        send_x_part(c, 1)

    def after_y(c):
        for d in range(2):
            pl.when(filled[2 * d])(lambda: y_copy(c, d).wait_recv())
            send_x_part(c, 2 * d)

    def after_x(c):
        for d in range(2):
            for dt in range(3):
                pl.when(sides[1 - d][0] & filled[dt])(lambda: x_copy(c, d, dt).wait_recv())

    def corner_copy(c, d, side):
        which, first, count = CHUNKS[c]
        source = kv.at[which, 1, 3 * side, pl.ds(first, count)]
        target = kv.at[which, 2 * d, 3 * side, pl.ds(first, count)]
        i = ROWS_FIRST.index(c)
        return pltpu.make_async_remote_copy(
            source, target, send_c.at[i, d, side], recv_c.at[i, d, side], device_id=times[d][1], device_id_type=MESH)

    def send_corners(c):
        for side in range(2):
            here = sides[1 - side][0]
            pl.when(here)(lambda: x_copy(c, side, 1).wait_recv())
            for d in range(2):
                pl.when(here & times[d][0])(lambda: corner_copy(c, d, side).start())

    def own_y_here(c):
        for d in range(2):
            pl.when(filled[2 * d])(lambda: y_copy(c, d).wait_recv())

    def corners_here(c):
        for side in range(2):
            for d in range(2):
                pl.when(sides[1 - side][0] & filled[2 * d])(lambda: corner_copy(c, d, side).wait_recv())

    def queries_here(i):
        first, count = QUERY_GROUPS[i]
        whole = qs.at[:, pl.ds(first, count)]
        pltpu.make_async_copy(whole, whole, recv_q.at[i]).wait()

    limits = []
    for row in range(4):
        tile = 2 * me.x - 1 + row
        inside = (tile >= 0) & (tile < 8)
        limits.append(jnp.where(inside, row_valid[jnp.clip(tile, 0, 7)], 0))

    def attend(wave, r, slot, base, count, column, first):
        off_t, off_r, off_c = [offsets[me.t, i, column, 2 * me.x + r] for i in range(3)]
        query = qs[r, slot].reshape(256, HEAD_DIM)
        if wave == 0:
            near = [(1, 1, limits[1]), (1, 2, limits[2])]
        elif wave == 1:
            near = [(dt, row, limits[row]) for dt in (0, 2) for row in (1, 2)]
        else:
            near = [(dt, 3 * r, jnp.where(r == 0, limits[0], limits[3])) for dt in (0, 1, 2)]
        less = []
        for dt, row, valid in near:
            dr = row - r - 1
            ok = ((dt - 1) * off_t >= 0) & (dr * off_r >= 0)
            if dt != 1:
                ok = ok & filled[dt]
            for j in range(count):
                limit = jnp.where(ok & ((first + j) * off_c >= 0), valid, 0)
                less.append([jnp.where(limit > row_in, 0.0, -jnp.inf).astype(F32) for row_in in range(8)])
        best = jnp.full((8, 256), -jnp.inf, F32)
        for i, (dt, row, _) in enumerate(near):
            for j in range(count):
                keys = kv[0, dt, row, base + j].reshape(256, HEAD_DIM)
                s = lax.dot_general(keys, query, (((1,), (1,)), ((), ())), preferred_element_type=F32)
                scores[3 - count, i, pl.ds(j * 256, 256)] = s
                highest = jnp.max(s.reshape(8, 4, 8, 256), axis=1)
                for n in range(8):
                    best = jnp.maximum(best, highest[n] + less[i * count + j][n])
        return lambda: weigh(wave, r, slot, base, count, near, less, best)

    def weigh(wave, r, slot, base, count, near, less, best):
        best = jnp.broadcast_to(jnp.max(best, axis=0, keepdims=True), (8, 256))
        if wave == 0:
            summed = jnp.zeros((8, 256), F32)
            held = jnp.zeros((HEAD_DIM, 256), F32)
        else:
            before = top[r, slot]
            best = jnp.maximum(best, before)
            fade = jnp.exp2((before - best) * SCALE)
            summed = total[r, slot] * fade
            held = gathered[r, slot] * fade[0:1]
        shift = best * SCALE
        for i, (dt, row, _) in enumerate(near):
            for j in range(count):
                parts = []
                for n in range(8):
                    s = scores[3 - count, i, pl.ds(j * 256 + n * 32, 32)].reshape(4, 8, 256)
                    p = jnp.exp2(s * SCALE - (shift - less[i * count + j][n])[None])
                    summed = summed + jnp.sum(p, axis=0)
                    parts.append(p.reshape(32, 256).astype(BF16))
                weights = jnp.concatenate(parts, axis=0)
                value = kv[1, dt, row, base + j].reshape(256, HEAD_DIM)
                held = held + lax.dot_general(value, weights, (((0,), (0,)), ((), ())), preferred_element_type=F32)
        if wave < 2:
            top[r, slot] = best
            total[r, slot] = summed
            gathered[r, slot] = held
        else:
            result = held / jnp.sum(summed, axis=0, keepdims=True)
            result = result.T.reshape(8, 32, HEAD_DIM)
            keep = lax.broadcasted_iota(jnp.int32, (8, 1, HEAD_DIM), 0) < jnp.where(r == 0, limits[1], limits[2])
            tiles[r, slot] = jnp.where(keep, result, 0.0).astype(BF16)

    def whole_head(wave, then=None):
        def step(r, _):
            def half(right, _):
                wide = attend(wave, r, 1 + right, right, 3, 1 + right, -1)
                edge = attend(wave, r, 3 * right, 2 * right, 2, 3 * right, -right)
                wide()
                edge()
                return 0

            lax.fori_loop(0, 2, half, 0)
            if then is not None:
                then(r)
            return 0

        lax.fori_loop(0, 2, step, 0)

    def shared_head(wave, then=None):
        def step(r, _):
            wide = attend(wave, r, 5 - me.zl, 4, 3, 1 + me.zl, -1)
            edge = attend(wave, r, 4 + me.zl, 4 + me.zl, 2, 3 * me.zl, -me.zl)
            wide()
            edge()
            if then is not None:
                then(r)
            return 0

        lax.fori_loop(0, 2, step, 0)

    def result_share(part, r, j):
        zp, core = rem(me.zp + div(j, 2), 2), rem(me.core + rem(j, 2), 2)
        device = (me.core * 8 + me.y * 2 + core, me.x * 4 + r * 2 + zp)
        rows, spot = pl.ds(zp * 4, 4), pl.ds(pl.multiple_of(core * 16, 16), 16)
        if part == 0:
            source = tiles.at[r, pl.ds(0, 4), rows, spot]
            target = landed.at[3 * me.zh + 2 * me.zl]
        else:
            source = tiles.at[r, pl.ds(4, 2), rows, spot]
            target = landed.at[3 * me.zh + 1, pl.ds(2 * me.zl, 2)]
        return source, target, pltpu.make_async_remote_copy(
            source, target, send_o.at[part, r, j], recv_o.at[part], device_id=device, device_id_type=MESH)

    def give_back(part, r):
        mine = myself & (r == me.zz)
        source, target, remote = result_share(part, r, jnp.int32(0))

        @pl.when(mine)
        def _():
            pltpu.make_async_copy(source, target, recv_o.at[part]).start()

        @pl.when(jnp.logical_not(mine))
        def _():
            remote.start()

        def step(j, _):
            result_share(part, r, j)[2].start()
            return 0

        lax.fori_loop(1, 4, step, 0)

    def given_back(part):
        def each(r, _):
            mine = myself & (r == me.zz)
            pl.when(jnp.logical_not(mine))(lambda: result_share(part, r, jnp.int32(0))[2].wait_send())

            def step(j, _):
                result_share(part, r, j)[2].wait_send()
                return 0

            lax.fori_loop(1, 4, step, 0)
            return 0

        lax.fori_loop(0, 2, each, 0)

    def landed_here(part):
        whole = landed.at[pl.ds(0, 8 if part == 0 else 4)]
        pltpu.make_async_copy(whole, whole, recv_o.at[part]).wait()

    pack(0, k_in)
    pl.semaphore_wait(barrier, expect)
    spread(*chunk_share(0))
    pack(1, v_in)
    spread(*chunk_share(1))
    spread(*chunk_share(2))
    spread(*chunk_share(3))
    pack(2, q_in)
    spread(*query_share(0))
    for c in range(4, 8):
        spread(*chunk_share(c))
    spread(*query_share(1))
    for c in range(4):
        after_own(c)
        if c:
            after_y(c - 1)
    after_y(3)
    queries_here(0)
    whole_head(0)

    def keys_on(r):
        @pl.when(r == 0)
        def _():
            after_own(4)
            after_own(5)

    whole_head(1, keys_on)
    send_corners(4)
    after_own(6)
    for c in range(4):
        after_x(c)

    def values_on(r):
        give_back(0, r)

        @pl.when(r == 0)
        def _():
            after_y(5)
            after_own(7)

    whole_head(2, values_on)
    send_corners(6)
    queries_here(1)
    shared_head(0)
    after_y(7)
    own_y_here(4)
    own_y_here(6)
    shared_head(1)
    after_x(5)
    after_x(7)
    corners_here(4)
    corners_here(6)
    shared_head(2, lambda r: give_back(1, r))
    landed_here(0)
    landed_here(1)
    for c in range(8):
        spread_sent(*chunk_share(c))
        for d in range(2):
            pl.when(times[d][0])(lambda: y_copy(c, d).wait_send())
            for dt in ((1,) if c in ROWS_FIRST else range(3)):
                pl.when(sides[d][0] & filled[dt])(lambda: x_copy(c, d, dt).wait_send())
            if c in ROWS_FIRST:
                for side in range(2):
                    pl.when(sides[1 - side][0] & times[d][0])(lambda: corner_copy(c, d, side).wait_send())
    for i in range(2):
        spread_sent(*query_share(i))
    for i in range(2):
        given_back(i)


def unpack_kernel(landed, out):
    for h in range(HEADS):
        block = landed[h].astype(F32).reshape(4, 4, 2, 8, HEAD_DIM)
        block = jnp.transpose(block, (2, 1, 0, 3, 4)).reshape(2, 4, 32, HEAD_DIM)
        out[:, :, :, h * HEAD_DIM:(h + 1) * HEAD_DIM] = block.astype(BF16)


def shards(queries, keys, values, win_off, row_valid):
    dma = pltpu.SemaphoreType.DMA
    smem = pl.BlockSpec(memory_space=pltpu.SMEM)
    vmem = pl.BlockSpec(memory_space=pltpu.VMEM)
    landed = pl.pallas_call(
        kernel,
        out_shape=jax.ShapeDtypeStruct((HEADS, 4, 4, 16, HEAD_DIM), BF16),
        in_specs=[smem, smem, vmem, vmem, vmem],
        out_specs=pl.BlockSpec(memory_space=pl.ANY),
        scratch_shapes=[
            pltpu.VMEM((2, 3, 4, 7, 8, 32, HEAD_DIM), BF16),
            pltpu.VMEM((2, 6, 8, 32, HEAD_DIM), BF16),
            pltpu.VMEM((3, HEADS, 4, 4, 16, HEAD_DIM), BF16),
            pltpu.VMEM((2, 6, 8, 32, HEAD_DIM), BF16),
            pltpu.VMEM((2, 4, 768, 256), F32),
            pltpu.VMEM((2, 6, 8, 256), F32),
            pltpu.VMEM((2, 6, 8, 256), F32),
            pltpu.VMEM((2, 6, HEAD_DIM, 256), F32),
            dma((8, 8)), dma((2, 8)), dma((8, 2)), dma((8, 2, 3)), dma((2, 2, 2)), dma((2, 2, 4)),
            dma((8,)), dma((2,)), dma((8, 2)), dma((8, 2, 3)), dma((2, 2, 2)), dma((2,)),
        ],
        compiler_params=pltpu.CompilerParams(
            collective_id=0, has_side_effects=True, vmem_limit_bytes=VMEM_LIMIT),
    )(jnp.transpose(win_off, (0, 3, 2, 1)), row_valid, queries, keys, values)
    return pl.pallas_call(
        unpack_kernel,
        out_shape=jax.ShapeDtypeStruct(queries.shape, BF16),
        in_specs=[vmem],
        out_specs=vmem,
    )(landed)


def solution(mesh):
    return jax.shard_map(
        shards,
        mesh=mesh,
        in_specs=(
            P("tm", "rows", None, None),
            P("tm", "rows", None, None),
            P("tm", "rows", None, None),
            P(),
            P(),
        ),
        out_specs=P("tm", "rows", None, None),
        check_vma=False,
    )
```

```python
import jax
import jax.numpy as jnp
from jax import lax
from jax.experimental import pallas as pl
from jax.experimental.pallas import tpu as pltpu
from jax.sharding import PartitionSpec as P

HEADS = 12
HEAD_DIM = 128
LOG2E = 1.4426950408889634
SCALE = LOG2E / HEAD_DIM**0.5
BF16 = jnp.bfloat16
F32 = jnp.float32
MESH = pl.DeviceIdType.MESH
VMEM_LIMIT = 60 * 1024 * 1024


def rem(a, b):
    return lax.rem(a, jnp.int32(b))


def div(a, b):
    return lax.div(a, jnp.int32(b))


class Place:
    def __init__(self):
        tm = lax.axis_index("tm")
        rows = lax.axis_index("rows")
        self.zl = div(tm, 8)
        self.y = rem(div(tm, 2), 4)
        self.core = rem(tm, 2)
        self.x = div(rows, 4)
        self.zh = rem(rows, 4)
        self.zz = div(self.zh, 2)
        self.zp = rem(self.zh, 2)
        self.z = self.zh * 2 + self.zl
        self.t = self.core * 4 + self.y
        self.rows = rows

    def worker(self, k):
        z = rem(self.z + k, 8)
        zh, zl = div(z, 2), rem(z, 2)
        return zh, zl, (zl * 8 + self.y * 2 + self.zl, self.x * 4 + zh)

    def origin(self, k):
        i = rem(self.z + k, 8)
        zh = rem(self.zh + k // 2, 4)
        core = rem(self.core + k % 2, 2)
        return zh, core, (self.core * 8 + self.y * 2 + core, self.x * 4 + zh)

    def time_neighbour(self, step):
        t = self.t + step
        ok = (t >= 0) & (t < 8)
        t = jnp.clip(t, 0, 7)
        return ok, (self.zl * 8 + rem(t, 4) * 2 + div(t, 4), self.rows)

    def row_neighbour(self, step):
        x = self.x + step
        ok = (x >= 0) & (x < 4)
        x = jnp.clip(x, 0, 3)
        return ok, (self.zl * 8 + self.y * 2 + self.core, x * 4 + self.zh)


GROUPS = ((0, 2), (2, 2), (6, 1), (4, 2))
CHUNKS = tuple((which, first, count) for which, (first, count) in (
    (0, GROUPS[0]), (1, GROUPS[0]), (0, GROUPS[1]), (1, GROUPS[1]),
    (0, GROUPS[2]), (0, GROUPS[3]), (1, GROUPS[2]), (1, GROUPS[3])))
QUERY_GROUPS = ((0, 4), (4, 2))
ROWS_FIRST = (4, 6)


def kernel(offsets, row_valid, q_in, k_in, v_in, landed, kv, qs, packed, tiles, scores, top, total, gathered,
           send_kv, send_q, send_y, send_x, send_c, send_o, recv_kv, recv_q, recv_y, recv_x, recv_c, recv_o):
    me = Place()
    times = [me.time_neighbour(s) for s in (1, -1)]
    sides = [me.row_neighbour(s) for s in (1, -1)]
    myself = me.core == me.zl
    other = jnp.logical_not(myself)

    for i, dt in ((1, 0), (0, 2)):
        @pl.when(jnp.logical_not(times[i][0]))
        def _():
            kv[:, dt] = jnp.zeros((2, 4, 7, 8, 32, HEAD_DIM), BF16)
    for i, row in ((1, 0), (0, 3)):
        @pl.when(jnp.logical_not(sides[i][0]))
        def _():
            kv[:, :, row] = jnp.zeros((2, 3, 7, 8, 32, HEAD_DIM), BF16)

    barrier = pltpu.get_barrier_semaphore()

    def greet(device):
        pl.semaphore_signal(barrier, inc=1, device_id=device, device_id_type=MESH)

    @pl.when(other)
    def _():
        greet(me.origin(0)[2])
        greet(me.worker(0)[2])

    for k in range(1, 8):
        greet(me.origin(k)[2])
        greet(me.worker(k)[2])
    expect = 16 - 2 * myself.astype(jnp.int32)
    for ok, device in times + sides:
        @pl.when(ok)
        def _():
            greet(device)
        expect = expect + ok.astype(jnp.int32)

    def pack(which, source):
        for h in range(HEADS):
            block = source[:, :, :, h * HEAD_DIM:(h + 1) * HEAD_DIM].astype(F32)
            block = block.reshape(2, 4, 4, 8, HEAD_DIM)
            block = jnp.transpose(block, (2, 1, 0, 3, 4)).reshape(4, 4, 16, HEAD_DIM)
            packed[which, h] = block.astype(BF16)

    my_rows, my_spot = pl.ds(me.zp * 4, 4), pl.ds(pl.multiple_of(me.core * 16, 16), 16)

    def share(which, first, count, send, recv, k):
        zh, zl, device = me.worker(k)
        if first < 4:
            head, column = 3 * zh + 2 * zl, first
        else:
            head, column = 3 * zh + 1, (2 * zl if which == 2 else zl) + first - 4
        source = packed.at[which, head, pl.ds(column, count)]
        if which == 2:
            target = qs.at[me.zz, pl.ds(first, count), my_rows, my_spot]
        else:
            target = kv.at[which, 1, 1 + me.zz, pl.ds(first, count), my_rows, my_spot]
        return source, target, pltpu.make_async_remote_copy(
            source, target, send.at[k], recv, device_id=device, device_id_type=MESH)

    def spread(which, first, count, send, recv):
        source, target, remote = share(which, first, count, send, recv, 0)

        @pl.when(myself)
        def _():
            pltpu.make_async_copy(source, target, recv).start()

        @pl.when(other)
        def _():
            remote.start()

        def step(k, _):
            share(which, first, count, send, recv, k)[2].start()
            return 0

        lax.fori_loop(1, 8, step, 0)

    def spread_sent(which, first, count, send, recv):
        pl.when(other)(lambda: share(which, first, count, send, recv, 0)[2].wait_send())

        def step(k, _):
            share(which, first, count, send, recv, k)[2].wait_send()
            return 0

        lax.fori_loop(1, 8, step, 0)

    def chunk_share(c):
        which, first, count = CHUNKS[c]
        return which, first, count, send_kv.at[c], recv_kv.at[c]

    def query_share(i):
        first, count = QUERY_GROUPS[i]
        return 2, first, count, send_q.at[i], recv_q.at[i]

    def y_copy(c, d):
        which, first, count = CHUNKS[c]
        source = kv.at[which, 1, pl.ds(1, 2), pl.ds(first, count)]
        target = kv.at[which, 2 * d, pl.ds(1, 2), pl.ds(first, count)]
        return pltpu.make_async_remote_copy(
            source, target, send_y.at[c, d], recv_y.at[c, d], device_id=times[d][1], device_id_type=MESH)

    def x_copy(c, d, dt):
        which, first, count = CHUNKS[c]
        source = kv.at[which, dt, 2 - d, pl.ds(first, count)]
        target = kv.at[which, dt, 3 * d, pl.ds(first, count)]
        return pltpu.make_async_remote_copy(
            source, target, send_x.at[c, d, dt], recv_x.at[c, d, dt], device_id=sides[d][1], device_id_type=MESH)

    filled = (times[1][0], True, times[0][0])

    def send_x_part(c, dt):
        for d in range(2):
            pl.when(sides[d][0] & filled[dt])(lambda: x_copy(c, d, dt).start())

    def after_own(c):
        which, first, count = CHUNKS[c]
        whole = kv.at[which, 1, pl.ds(1, 2), pl.ds(first, count)]
        pltpu.make_async_copy(whole, whole, recv_kv.at[c]).wait()
        for d in range(2):
            pl.when(times[d][0])(lambda: y_copy(c, d).start())
        send_x_part(c, 1)

    def after_y(c):
        for d in range(2):
            pl.when(filled[2 * d])(lambda: y_copy(c, d).wait_recv())
            send_x_part(c, 2 * d)

    def side_here(c, side):
        for dt in range(3):
            pl.when(sides[1 - side][0] & filled[dt])(lambda: x_copy(c, side, dt).wait_recv())

    def after_x(c):
        for side in range(2):
            side_here(c, side)

    def corner_copy(c, d, side):
        which, first, count = CHUNKS[c]
        source = kv.at[which, 1, 3 * side, pl.ds(first, count)]
        target = kv.at[which, 2 * d, 3 * side, pl.ds(first, count)]
        i = ROWS_FIRST.index(c)
        return pltpu.make_async_remote_copy(
            source, target, send_c.at[i, d, side], recv_c.at[i, d, side], device_id=times[d][1], device_id_type=MESH)

    def send_corners(c):
        for side in range(2):
            here = sides[1 - side][0]
            pl.when(here)(lambda: x_copy(c, side, 1).wait_recv())
            for d in range(2):
                pl.when(here & times[d][0])(lambda: corner_copy(c, d, side).start())

    def own_y_here(c):
        for d in range(2):
            pl.when(filled[2 * d])(lambda: y_copy(c, d).wait_recv())

    def corners_here(c, side):
        for d in range(2):
            pl.when(sides[1 - side][0] & filled[2 * d])(lambda: corner_copy(c, d, side).wait_recv())

    def shared_halo_here(side):
        side_here(5, side)
        corners_here(4, side)
        side_here(7, side)
        corners_here(6, side)

    def queries_here(i):
        first, count = QUERY_GROUPS[i]
        whole = qs.at[:, pl.ds(first, count)]
        pltpu.make_async_copy(whole, whole, recv_q.at[i]).wait()

    limits = []
    for row in range(4):
        tile = 2 * me.x - 1 + row
        inside = (tile >= 0) & (tile < 8)
        limits.append(jnp.where(inside, row_valid[jnp.clip(tile, 0, 7)], 0))

    def attend(wave, r, slot, base, count, column, first):
        off_t, off_r, off_c = [offsets[me.t, i, column, 2 * me.x + r] for i in range(3)]
        query = qs[r, slot].reshape(256, HEAD_DIM)
        if wave == 0:
            near = [(1, 1, limits[1]), (1, 2, limits[2])]
        elif wave == 1:
            near = [(dt, row, limits[row]) for dt in (0, 2) for row in (1, 2)]
        else:
            near = [(dt, 3 * r, jnp.where(r == 0, limits[0], limits[3])) for dt in (0, 1, 2)]
        less = []
        for dt, row, valid in near:
            dr = row - r - 1
            ok = ((dt - 1) * off_t >= 0) & (dr * off_r >= 0)
            if dt != 1:
                ok = ok & filled[dt]
            for j in range(count):
                limit = jnp.where(ok & ((first + j) * off_c >= 0), valid, 0)
                less.append([jnp.where(limit > row_in, 0.0, -jnp.inf).astype(F32) for row_in in range(8)])
        best = jnp.full((8, 256), -jnp.inf, F32)
        for i, (dt, row, _) in enumerate(near):
            for j in range(count):
                keys = kv[0, dt, row, base + j].reshape(256, HEAD_DIM)
                s = lax.dot_general(keys, query, (((1,), (1,)), ((), ())), preferred_element_type=F32)
                scores[3 - count, i, pl.ds(j * 256, 256)] = s
                highest = jnp.max(s.reshape(8, 4, 8, 256), axis=1)
                for n in range(8):
                    best = jnp.maximum(best, highest[n] + less[i * count + j][n])
        return lambda: weigh(wave, r, slot, base, count, near, less, best)

    def weigh(wave, r, slot, base, count, near, less, best):
        best = jnp.broadcast_to(jnp.max(best, axis=0, keepdims=True), (8, 256))
        if wave == 0:
            summed = jnp.zeros((8, 256), F32)
            held = jnp.zeros((HEAD_DIM, 256), F32)
        else:
            before = top[r, slot]
            best = jnp.maximum(best, before)
            fade = jnp.exp2((before - best) * SCALE)
            summed = total[r, slot] * fade
            held = gathered[r, slot] * fade[0:1]
        shift = best * SCALE
        for i, (dt, row, _) in enumerate(near):
            for j in range(count):
                parts = []
                for n in range(8):
                    s = scores[3 - count, i, pl.ds(j * 256 + n * 32, 32)].reshape(4, 8, 256)
                    p = jnp.exp2(s * SCALE - (shift - less[i * count + j][n])[None])
                    summed = summed + jnp.sum(p, axis=0)
                    parts.append(p.reshape(32, 256).astype(BF16))
                weights = jnp.concatenate(parts, axis=0)
                value = kv[1, dt, row, base + j].reshape(256, HEAD_DIM)
                held = held + lax.dot_general(value, weights, (((0,), (0,)), ((), ())), preferred_element_type=F32)
        if wave < 2:
            top[r, slot] = best
            total[r, slot] = summed
            gathered[r, slot] = held
        else:
            result = held / jnp.sum(summed, axis=0, keepdims=True)
            result = result.T.reshape(8, 32, HEAD_DIM)
            keep = lax.broadcasted_iota(jnp.int32, (8, 1, HEAD_DIM), 0) < jnp.where(r == 0, limits[1], limits[2])
            tiles[r, slot] = jnp.where(keep, result, 0.0).astype(BF16)

    def whole_head(wave, then=None):
        def step(r, _):
            def half(right, _):
                wide = attend(wave, r, 1 + right, right, 3, 1 + right, -1)
                edge = attend(wave, r, 3 * right, 2 * right, 2, 3 * right, -right)
                wide()
                edge()
                return 0

            lax.fori_loop(0, 2, half, 0)
            if then is not None:
                then(r)
            return 0

        lax.fori_loop(0, 2, step, 0)

    def shared_head(wave, then=None):
        def step(r, _):
            if wave == 2:
                for side in range(2):
                    pl.when(r == side)(lambda: shared_halo_here(side))
            wide = attend(wave, r, 5 - me.zl, 4, 3, 1 + me.zl, -1)
            edge = attend(wave, r, 4 + me.zl, 4 + me.zl, 2, 3 * me.zl, -me.zl)
            wide()
            edge()
            if then is not None:
                then(r)
            return 0

        lax.fori_loop(0, 2, step, 0)

    def result_share(part, r, j):
        zp, core = rem(me.zp + div(j, 2), 2), rem(me.core + rem(j, 2), 2)
        device = (me.core * 8 + me.y * 2 + core, me.x * 4 + r * 2 + zp)
        rows, spot = pl.ds(zp * 4, 4), pl.ds(pl.multiple_of(core * 16, 16), 16)
        if part == 0:
            source = tiles.at[r, pl.ds(0, 4), rows, spot]
            target = landed.at[3 * me.zh + 2 * me.zl]
        else:
            source = tiles.at[r, pl.ds(4, 2), rows, spot]
            target = landed.at[3 * me.zh + 1, pl.ds(2 * me.zl, 2)]
        return source, target, pltpu.make_async_remote_copy(
            source, target, send_o.at[part, r, j], recv_o.at[part], device_id=device, device_id_type=MESH)

    def give_back(part, r):
        mine = myself & (r == me.zz)
        source, target, remote = result_share(part, r, jnp.int32(0))

        @pl.when(mine)
        def _():
            pltpu.make_async_copy(source, target, recv_o.at[part]).start()

        @pl.when(jnp.logical_not(mine))
        def _():
            remote.start()

        def step(j, _):
            result_share(part, r, j)[2].start()
            return 0

        lax.fori_loop(1, 4, step, 0)

    def given_back(part):
        def each(r, _):
            mine = myself & (r == me.zz)
            pl.when(jnp.logical_not(mine))(lambda: result_share(part, r, jnp.int32(0))[2].wait_send())

            def step(j, _):
                result_share(part, r, j)[2].wait_send()
                return 0

            lax.fori_loop(1, 4, step, 0)
            return 0

        lax.fori_loop(0, 2, each, 0)

    def landed_here(part):
        whole = landed.at[pl.ds(0, 8 if part == 0 else 4)]
        pltpu.make_async_copy(whole, whole, recv_o.at[part]).wait()

    pack(0, k_in)
    pl.semaphore_wait(barrier, expect)
    spread(*chunk_share(0))
    pack(1, v_in)
    spread(*chunk_share(1))
    spread(*chunk_share(2))
    spread(*chunk_share(3))
    pack(2, q_in)
    spread(*query_share(0))
    for c in range(4, 8):
        spread(*chunk_share(c))
    spread(*query_share(1))
    for c in range(4):
        after_own(c)
        if c:
            after_y(c - 1)
    after_y(3)
    queries_here(0)
    whole_head(0)

    def keys_on(r):
        @pl.when(r == 0)
        def _():
            after_own(4)
            after_own(5)

    whole_head(1, keys_on)
    send_corners(4)
    after_own(6)
    for c in range(4):
        after_x(c)

    def values_on(r):
        give_back(0, r)

        @pl.when(r == 0)
        def _():
            after_y(5)
            after_own(7)

    whole_head(2, values_on)
    send_corners(6)
    queries_here(1)
    shared_head(0)
    after_y(7)
    own_y_here(4)
    own_y_here(6)
    shared_head(1)
    shared_head(2, lambda r: give_back(1, r))
    landed_here(0)
    landed_here(1)
    for c in range(8):
        spread_sent(*chunk_share(c))
        for d in range(2):
            pl.when(times[d][0])(lambda: y_copy(c, d).wait_send())
            for dt in ((1,) if c in ROWS_FIRST else range(3)):
                pl.when(sides[d][0] & filled[dt])(lambda: x_copy(c, d, dt).wait_send())
            if c in ROWS_FIRST:
                for side in range(2):
                    pl.when(sides[1 - side][0] & times[d][0])(lambda: corner_copy(c, d, side).wait_send())
    for i in range(2):
        spread_sent(*query_share(i))
    for i in range(2):
        given_back(i)


def unpack_kernel(landed, out):
    for h in range(HEADS):
        block = landed[h].astype(F32).reshape(4, 4, 2, 8, HEAD_DIM)
        block = jnp.transpose(block, (2, 1, 0, 3, 4)).reshape(2, 4, 32, HEAD_DIM)
        out[:, :, :, h * HEAD_DIM:(h + 1) * HEAD_DIM] = block.astype(BF16)


def shards(queries, keys, values, win_off, row_valid):
    dma = pltpu.SemaphoreType.DMA
    smem = pl.BlockSpec(memory_space=pltpu.SMEM)
    vmem = pl.BlockSpec(memory_space=pltpu.VMEM)
    landed = pl.pallas_call(
        kernel,
        out_shape=jax.ShapeDtypeStruct((HEADS, 4, 4, 16, HEAD_DIM), BF16),
        in_specs=[smem, smem, vmem, vmem, vmem],
        out_specs=pl.BlockSpec(memory_space=pl.ANY),
        scratch_shapes=[
            pltpu.VMEM((2, 3, 4, 7, 8, 32, HEAD_DIM), BF16),
            pltpu.VMEM((2, 6, 8, 32, HEAD_DIM), BF16),
            pltpu.VMEM((3, HEADS, 4, 4, 16, HEAD_DIM), BF16),
            pltpu.VMEM((2, 6, 8, 32, HEAD_DIM), BF16),
            pltpu.VMEM((2, 4, 768, 256), F32),
            pltpu.VMEM((2, 6, 8, 256), F32),
            pltpu.VMEM((2, 6, 8, 256), F32),
            pltpu.VMEM((2, 6, HEAD_DIM, 256), F32),
            dma((8, 8)), dma((2, 8)), dma((8, 2)), dma((8, 2, 3)), dma((2, 2, 2)), dma((2, 2, 4)),
            dma((8,)), dma((2,)), dma((8, 2)), dma((8, 2, 3)), dma((2, 2, 2)), dma((2,)),
        ],
        compiler_params=pltpu.CompilerParams(
            collective_id=0, has_side_effects=True, vmem_limit_bytes=VMEM_LIMIT),
    )(jnp.transpose(win_off, (0, 3, 2, 1)), row_valid, queries, keys, values)
    return pl.pallas_call(
        unpack_kernel,
        out_shape=jax.ShapeDtypeStruct(queries.shape, BF16),
        in_specs=[vmem],
        out_specs=vmem,
    )(landed)


def solution(mesh):
    return jax.shard_map(
        shards,
        mesh=mesh,
        in_specs=(
            P("tm", "rows", None, None),
            P("tm", "rows", None, None),
            P("tm", "rows", None, None),
            P(),
            P(),
        ),
        out_specs=P("tm", "rows", None, None),
        check_vma=False,
    )
```
